128 devices in a mesh: pb: 8 (over y, core), pa: 16 (over z, x).
Axes of the slice: x: 4, y: 4, z: 4, core: 2. Of those that a mesh axis runs over, the one named last changes fastest.
Arguments:
- queries: bfloat16 [65536, 4096], P(('pb', 'pa')), may hold values from -32 to 32
- passages: bfloat16 [65536, 4096], P(('pb', 'pa')), may hold values from -32 to 32
- cluster_sizes: int32 [64], replicated, may hold values from 1 to 3, 128 in all
- positives: int32 [128, 512], P(('pb', 'pa')), may hold values from 0 to 511, each once within a row
Outputs:
- grad_queries: bfloat16 [65536, 4096], P(('pb', 'pa'))
- grad_passages: bfloat16 [65536, 4096], P(('pb', 'pa'))
- row_losses: float32 [128, 512], P(('pb', 'pa'))
The draws below stay inside these ranges and needn't reach their ends.
Inputs may be any that keep to these rules, and one draw needn't show every extreme that they name: `cluster_sizes`: the sizes add up to 128. `positives`: each block's list names every row of 0 to 511 once.
All inputs are finite; a program needn't handle non-finite values.
Results may differ from the reference program's by a relative error of at most 0.0051.
Values may be sent and summed in bfloat16 or wider, within the bound.
A program may use at most 256 MiB of HBM per device.

```python
import math
import jax
import jax.numpy as jnp
import numpy as np
from jax import lax

D = 4096
BLK = 512
KMAX = 3
NB = 128
NCL = 64
NQ = 65536


def passage_field(key, lowest_scale, highest_scale):
    noise_rows = jax.random.normal(jax.random.fold_in(key, 101), (NB, BLK, D), jnp.float32)
    spread = jax.random.uniform(jax.random.fold_in(key, 102), (NB, BLK, 1), jnp.float32)
    scales = jnp.exp(jnp.log(lowest_scale) + spread * (jnp.log(highest_scale) - jnp.log(lowest_scale)))
    base_rows = noise_rows * scales
    field = base_rows
    return field


def draw_passages(key, part):
    field = passage_field(key, 0.7, 1.4)
    return jnp.clip(field, -32.0, 32.0).reshape(NB * BLK, D).astype(jnp.bfloat16)


def draw_queries(key, part):
    lowest_scale, highest_scale = (0.7, 1.4)
    own_key = jax.random.fold_in(key, 5)
    noise_rows = jax.random.normal(jax.random.fold_in(own_key, 1), (NB, BLK, D), jnp.float32)
    spread = jax.random.uniform(jax.random.fold_in(own_key, 2), (NB, BLK, 1), jnp.float32)
    scales = jnp.exp(jnp.log(lowest_scale) + spread * (jnp.log(highest_scale) - jnp.log(lowest_scale)))
    base_rows = noise_rows * scales
    field = base_rows
    return jnp.clip(field, -32.0, 32.0).reshape(NB * BLK, D).astype(jnp.bfloat16)


def profile(number_of, total, reach, skew):
    portions = [(1 << 20) // math.isqrt(standing ** skew) + 1 for standing in range(2, number_of + 1)]
    spare, holding = total - reach - (number_of - 1), [1] * (number_of - 1)
    while spare > 0:
        movable = [i for i in range(number_of - 1) if holding[i] < reach]
        whole, budget = sum([portions[i] for i in movable]), spare
        for i in movable:
            addition = min(reach - holding[i], max(1, budget * portions[i] // whole), spare)
            holding[i] = holding[i] + addition
            spare = spare - addition
    return np.array([reach] + holding)


def uneven(key, amount, total, limit, skew):
    if amount == 2:
        one = jax.random.randint(key, (), max(1, total - limit), min(limit, total - 1) + 1)
        return jnp.stack([one, total - one])
    tallies = jnp.asarray(profile(amount, total, limit, skew), jnp.int32)
    twos = (amount - 1) // 2
    giver, receiver = tallies[1:1 + 2 * twos:2], tallies[2:2 + 2 * twos:2]
    room = jnp.minimum(giver - 1, limit - receiver)
    shifted = jax.random.randint(jax.random.fold_in(key, 1), (twos,), 0, 1 << 20) % (room + 1)
    tallies = tallies.at[1:1 + 2 * twos:2].set(giver - shifted).at[2:2 + 2 * twos:2].set(receiver + shifted)
    return tallies[jax.random.permutation(jax.random.fold_in(key, 2), amount)]


def setup_inputs(seed: int = 0) -> dict:
    seeds = jax.random.split(jax.random.key(seed), 5)
    return {
        "queries": draw_queries(jax.random.fold_in(seeds[4], 71), 0),
        "passages": draw_passages(jax.random.fold_in(seeds[4], 71), 0),
        "cluster_sizes": uneven(seeds[2], NCL, NB, KMAX, 2).astype(jnp.int32),
        "positives": jax.vmap(lambda own: jax.random.permutation(own, BLK))(jax.random.split(seeds[3], NB)).reshape((NB, BLK)).astype(jnp.int32),
    }


LOWEST = -1.0e30


def cluster_index(cluster_sizes, block_count):
    cluster_ends = jnp.cumsum(cluster_sizes)
    blocks_all = jnp.arange(block_count, dtype=jnp.int32)
    return jnp.sum((cluster_ends[None, :] <= blocks_all[:, None]).astype(jnp.int32), axis=1)


def take_block(blocks_all, position):
    clipped = jnp.clip(position, 0, blocks_all.shape[0] - 1).astype(jnp.int32)
    return lax.dynamic_index_in_dim(blocks_all, clipped, 0, keepdims=False)


def linked(cluster_of, first, second):
    in_range = jnp.logical_and(second >= 0, second < cluster_of.shape[0])
    return jnp.logical_and(in_range, take_block(cluster_of, second) == take_block(cluster_of, first))


def score_pair(query_block, passage_block):
    product = lax.dot_general(query_block, passage_block, (((1,), (1,)), ((), ())), preferred_element_type=jnp.float32)
    return product * (D ** -0.5)


def masked_scores(linked_now, query_block, passage_block):
    return lax.cond(linked_now, lambda: score_pair(query_block, passage_block), lambda: jnp.zeros((BLK, BLK), jnp.float32))


def grad_weights(block_scores, row_lse, column_lse, linked_now, onehot):
    weight_values = jnp.exp(block_scores - row_lse[:, None]) + jnp.exp(block_scores - column_lse[None, :])
    if onehot is not None:
        weight_values = jnp.where(onehot, weight_values - 2.0, weight_values)
    return jnp.where(linked_now, weight_values, 0.0).astype(jnp.bfloat16)


def reference(queries, passages, cluster_sizes, positives):
    reach_most = KMAX - 1
    offsets = list(range(-reach_most, reach_most + 1))
    cluster_of = cluster_index(cluster_sizes, NB)
    query_blocks = queries.reshape(NB, BLK, D)
    passage_blocks = passages.reshape(NB, BLK, D)
    columns = jnp.arange(BLK, dtype=jnp.int32)

    def first_pass(block_index):
        own_queries = take_block(query_blocks, block_index)
        row_max = jnp.full((BLK,), LOWEST, jnp.float32)
        collected = []
        for offset in offsets:
            partner_block = block_index - offset
            linked_now = linked(cluster_of, block_index, partner_block)
            block_scores = masked_scores(linked_now, own_queries, take_block(passage_blocks, partner_block))
            collected.append((linked_now, block_scores))
            row_max = jnp.maximum(row_max, jnp.where(linked_now, jnp.max(block_scores, axis=1), LOWEST))
        row_sum = jnp.zeros((BLK,), jnp.float32)
        column_max = []
        column_sum = []
        for linked_now, block_scores in collected:
            row_sum = row_sum + jnp.where(linked_now, jnp.sum(jnp.exp(block_scores - row_max[:, None]), axis=1), 0.0)
            column_peak = jnp.where(linked_now, jnp.max(block_scores, axis=0), LOWEST)
            column_max.append(column_peak)
            column_sum.append(jnp.where(linked_now, jnp.sum(jnp.exp(block_scores - column_peak[None, :]), axis=0), 0.0))
        return row_max + jnp.log(row_sum), jnp.stack(column_max), jnp.stack(column_sum)

    row_lse, column_max, column_sum = lax.map(first_pass, jnp.arange(NB, dtype=jnp.int32))
    padding_max = jnp.full((reach_most, len(offsets), BLK), LOWEST, jnp.float32)
    padding_sum = jnp.zeros((reach_most, len(offsets), BLK), jnp.float32)
    padded_max = jnp.concatenate([padding_max, column_max, padding_max], axis=0)
    padded_sum = jnp.concatenate([padding_sum, column_sum, padding_sum], axis=0)
    partials = []
    for position, offset in enumerate(offsets):
        first_row = reach_most + offset
        partials.append((padded_max[first_row:first_row + NB, position], padded_sum[first_row:first_row + NB, position]))
    merged_max = partials[0][0]
    for partial_value in partials[1:]:
        merged_max = jnp.maximum(merged_max, partial_value[0])
    merged_total = jnp.zeros((NB, BLK), jnp.float32)
    for partial_value in partials:
        merged_total = merged_total + partial_value[1] * jnp.exp(partial_value[0] - merged_max)
    column_lse = merged_max + jnp.log(merged_total)

    def second_pass(block_index):
        own_queries = take_block(query_blocks, block_index)
        own_row_lse = take_block(row_lse, block_index)
        onehot = take_block(positives, block_index)[:, None] == columns[None, :]
        accumulated = jnp.zeros((BLK, D), jnp.float32)
        row_loss = jnp.zeros((BLK,), jnp.float32)
        for offset in offsets:
            partner_block = block_index - offset
            linked_now = linked(cluster_of, block_index, partner_block)
            partner_passages = take_block(passage_blocks, partner_block)
            block_scores = masked_scores(linked_now, own_queries, partner_passages)
            partner_lse = take_block(column_lse, partner_block)
            weights = grad_weights(block_scores, own_row_lse, partner_lse, linked_now, onehot if offset == 0 else None)
            accumulated = accumulated + lax.cond(
                linked_now,
                lambda: jnp.dot(weights, partner_passages, preferred_element_type=jnp.float32),
                lambda: jnp.zeros((BLK, D), jnp.float32))
            if offset == 0:
                target = jnp.sum(jnp.where(onehot, block_scores, 0.0), axis=1)
                column_at = jnp.sum(jnp.where(onehot, partner_lse[None, :], 0.0), axis=1)
                row_loss = own_row_lse + column_at - 2.0 * target
        return accumulated.astype(jnp.bfloat16), row_loss

    def third_pass(block_index):
        own_passages = take_block(passage_blocks, block_index)
        own_column_lse = take_block(column_lse, block_index)
        onehot = take_block(positives, block_index)[:, None] == columns[None, :]
        accumulated = jnp.zeros((BLK, D), jnp.float32)
        for offset in offsets:
            partner_block = block_index + offset
            linked_now = linked(cluster_of, block_index, partner_block)
            partner_queries = take_block(query_blocks, partner_block)
            block_scores = masked_scores(linked_now, partner_queries, own_passages)
            weights = grad_weights(block_scores, take_block(row_lse, partner_block), own_column_lse, linked_now, onehot if offset == 0 else None)
            grad_term = lax.cond(
                linked_now,
                lambda: lax.dot_general(weights, partner_queries, (((0,), (0,)), ((), ())), preferred_element_type=jnp.float32).astype(jnp.bfloat16),
                lambda: jnp.zeros((BLK, D), jnp.bfloat16))
            accumulated = accumulated + lax.optimization_barrier(grad_term).astype(jnp.float32)
        return accumulated.astype(jnp.bfloat16)

    block_ids = jnp.arange(NB, dtype=jnp.int32)
    grad_rows, row_losses = lax.map(second_pass, block_ids)
    grad_columns = lax.map(third_pass, block_ids)
    return grad_rows.reshape(NQ, D), grad_columns.reshape(NQ, D), row_losses
```

```python
import jax
import jax.numpy as jnp
from jax import lax
from jax.experimental import pallas as pl
from jax.experimental.pallas import tpu as pltpu
from jax.sharding import PartitionSpec as P

BLK = 512
D = 4096
NB = 128
NCL = 64
NC = 8
CW = D // NC
PA = 16
HALVES = 2
VM = 62
HB = BLK // HALVES
LOWEST = -1e30
SCALE = float(D) ** (-0.5)
F32 = jnp.float32
BF16 = jnp.bfloat16
MESH = pl.DeviceIdType.MESH


def dot_nt(a, b):
    return lax.dot_general(a, b, (((1,), (1,)), ((), ())), preferred_element_type=F32)


def dot_nn(a, b):
    return jnp.dot(a, b, preferred_element_type=F32)


def mask_of(flag, shape):
    return jnp.full(shape, flag, jnp.int32) > 0


def exchange_kernel(
    sizes_ref, pos_ref, q_hbm, p_hbm,
    gq_hbm, gp_hbm, loss_ref,
    q0, p0, pl_in, pr_in, xl_in, xr_in, tl_in, tr_in, send_r, send_l,
    s3, row_lse, col_lse, msg_l, msg_r, pos_t, w_row, wt_p, stage,
    sem_q, sem_p, ps_r, ps_l, pr_r, pr_l, xs_r, xs_l, xr_r, xr_l, ts_r, ts_l, tr_r, tr_l,
    msg_send, msg_recv, out_sem,
):
    pb, pa = lax.axis_index("pb"), lax.axis_index("pa")
    me = pb * PA + pa
    after = lax.rem(me + 1, NB)
    before = lax.rem(me + NB - 1, NB)
    right = (after // PA, lax.rem(after, PA))
    left = (before // PA, lax.rem(before, PA))

    barrier = pltpu.get_barrier_semaphore()
    for neighbour in (left, right):
        pl.semaphore_signal(barrier, inc=1, device_id=neighbour, device_id_type=MESH)
    pl.semaphore_wait(barrier, 2)

    def columns(c):
        return pl.ds(pl.multiple_of(c * CW, CW), CW)

    def remote(src, dst, send, recv, to):
        return pltpu.make_async_remote_copy(
            src_ref=src, dst_ref=dst, send_sem=send, recv_sem=recv, device_id=to, device_id_type=MESH
        )

    def p_right(c):
        return remote(p_hbm.at[:, columns(c)], pl_in.at[c], ps_r.at[c], pr_r.at[c], right)

    def p_left(c):
        return remote(p_hbm.at[:, columns(c)], pr_in.at[c], ps_l.at[c], pr_l.at[c], left)

    def x_right(c):
        return remote(send_r.at[c], xl_in.at[c], xs_r.at[c], xr_r.at[c], right)

    def x_left(c):
        return remote(send_l.at[c], xr_in.at[c], xs_l.at[c], xr_l.at[c], left)

    def t_right(c):
        return remote(send_r.at[c], tl_in.at[c], ts_r.at[c], tr_r.at[c], right)

    def t_left(c):
        return remote(send_l.at[c], tr_in.at[c], ts_l.at[c], tr_l.at[c], left)

    def q_load(c):
        return pltpu.make_async_copy(q_hbm.at[:, columns(c)], q0.at[c], sem_q.at[c])

    def p_load(c):
        return pltpu.make_async_copy(p_hbm.at[:, columns(c)], p0.at[c], sem_p.at[c])

    @pl.loop(0, NC)
    def _(c):
        p_right(c).start()
        p_left(c).start()
        q_load(c).start()
        p_load(c).start()

    def scan_sizes(k, carry):
        end, at_me, at_next, at_before, at_after = carry
        end = end + sizes_ref[k]
        one = jnp.int32(1)
        return (
            end,
            jnp.where(end == me, one, at_me),
            jnp.where(end == me + 1, one, at_next),
            jnp.where(end == me - 1, one, at_before),
            jnp.where(end == me + 2, one, at_after),
        )

    zero = jnp.int32(0)
    _, at_me, at_next, at_before, at_after = lax.fori_loop(0, NCL, scan_sizes, (zero,) * 5)
    has_l = jnp.where(me > 0, 1 - at_me, 0)
    has_r = jnp.where(me < NB - 1, 1 - at_next, 0)
    far_l = jnp.where(me > 1, 1 - at_before, 0) * has_l
    far_r = jnp.where(me < NB - 2, 1 - at_after, 0) * has_r
    rows_l = has_l - far_l
    rows_r = has_r - far_r

    def add_scores(r, k, c, a_ref, b_ref):
        for h in range(HALVES):
            ref = s3.at[pl.ds(r * BLK + h * HB, HB), pl.ds(k * BLK, BLK)]
            part = dot_nt(a_ref[c, h * HB:(h + 1) * HB, :], b_ref[c])

            @pl.when(c == 0)
            def _():
                ref[...] = part

            @pl.when(c > 0)
            def _():
                ref[...] += part

    @pl.loop(0, NC)
    def _(c):
        q_load(c).wait()
        p_load(c).wait()
        add_scores(1, 1, c, q0, p0)

    @pl.loop(0, NC)
    def _(c):
        p_right(c).wait_recv()
        p_left(c).wait_recv()
        for h in range(HALVES):
            here = slice(h * HB, (h + 1) * HB)
            send_r[c, here, :] = jnp.where(mask_of(has_l, (HB, CW)), pl_in[c, here, :], q0[c, here, :])
        x_right(c).start()
        for h in range(HALVES):
            here = slice(h * HB, (h + 1) * HB)
            send_l[c, here, :] = jnp.where(mask_of(has_r, (HB, CW)), pr_in[c, here, :], q0[c, here, :])
        x_left(c).start()
        add_scores(1, 0, c, q0, pl_in)
        add_scores(1, 2, c, q0, pr_in)

    @pl.loop(0, NC)
    def _(c):
        x_right(c).wait_recv()
        x_left(c).wait_recv()
        for r, x_in in ((0, xl_in), (2, xr_in)):
            for k, p_in in ((0, pl_in), (1, p0), (2, pr_in)):
                add_scores(r, k, c, x_in, p_in)

    held_rows = (rows_l, jnp.int32(1), rows_r)
    held_cols = (has_l, jnp.int32(1), has_r)
    RT = 64

    def valid(r, k, shape):
        return mask_of(held_rows[r] * held_cols[k], shape)

    col_peak = [jnp.full((8, BLK), LOWEST, F32) for _ in range(3)]
    for r in range(3):
        def peaks(t, peak):
            rows = pl.ds(pl.multiple_of(r * BLK + t * RT, RT), RT)
            tiles = [
                jnp.where(valid(r, k, (RT, BLK)), s3[rows, k * BLK:(k + 1) * BLK] * SCALE, LOWEST)
                for k in range(3)
            ]
            top = jnp.max(jnp.maximum(jnp.maximum(tiles[0], tiles[1]), tiles[2]), axis=1, keepdims=True)
            total = jnp.zeros((RT, 1), F32)
            for tile in tiles:
                total = total + jnp.sum(jnp.exp(tile - top), axis=1, keepdims=True)
            row_lse[rows, :] = jnp.broadcast_to(top + jnp.log(total), (RT, 128))
            return tuple(
                jnp.maximum(old, jnp.max(tile.reshape(RT // 8, 8, BLK), axis=0))
                for old, tile in zip(peak, tiles)
            )

        col_peak = lax.fori_loop(0, BLK // RT, peaks, tuple(col_peak))
    col_top = [jnp.max(peak, axis=0, keepdims=True) for peak in col_peak]
    col_sum = [jnp.zeros((8, BLK), F32) for _ in range(3)]
    for r in range(3):
        def sums(t, total):
            rows = pl.ds(pl.multiple_of(r * BLK + t * RT, RT), RT)
            out = []
            for k in range(3):
                tile = jnp.where(valid(r, k, (RT, BLK)), s3[rows, k * BLK:(k + 1) * BLK] * SCALE, LOWEST)
                part = jnp.exp(tile - col_top[k])
                out.append(total[k] + jnp.sum(part.reshape(RT // 8, 8, BLK), axis=0))
            return tuple(out)

        col_sum = lax.fori_loop(0, BLK // RT, sums, tuple(col_sum))
    for k in range(3):
        lse = col_top[k] + jnp.log(jnp.sum(col_sum[k], axis=0, keepdims=True))
        col_lse[:, k * BLK:(k + 1) * BLK] = jnp.broadcast_to(lse, (8, BLK))

    tell_r = remote(col_lse, msg_l, msg_send.at[0], msg_recv.at[0], right)
    tell_l = remote(col_lse, msg_r, msg_send.at[1], msg_recv.at[1], left)
    tell_r.start()
    tell_l.start()

    def weight_tile(tile, lse_rows, lse_cols):
        return jnp.exp(tile - lse_rows) + jnp.exp(tile - lse_cols)

    def weights_t(r, k, out, at):
        ok = held_rows[r] * held_cols[k]
        lse_cols = col_lse[0:1, k * BLK:(k + 1) * BLK]

        @pl.loop(0, 4)
        def _(t):
            rows = pl.ds(pl.multiple_of(r * BLK + t * 128, 128), 128)
            tile = s3[rows, k * BLK:(k + 1) * BLK] * SCALE
            value = weight_tile(tile, row_lse[rows, 0:1], lse_cols)
            value = jnp.where(mask_of(ok, value.shape), value, 0.0)
            out[:, pl.ds(pl.multiple_of(at + t * 128, 128), 128)] = value.T.astype(BF16)

    for place, (r, k) in enumerate(((1, 0), (2, 0), (1, 2), (0, 2))):
        weights_t(r, k, w_row, place * BLK)

    @pl.loop(0, NC)
    def _(c):
        x_left(c).wait_send()
        for h in range(HALVES):
            here = slice(h * HB, (h + 1) * HB)
            term = dot_nn(w_row[here, :BLK], q0[c]) + dot_nn(w_row[here, BLK:2 * BLK], xr_in[c])
            send_l[c, here, :] = term.astype(BF16)
        t_left(c).start()
        x_right(c).wait_send()
        for h in range(HALVES):
            here = slice(h * HB, (h + 1) * HB)
            term = dot_nn(w_row[here, 2 * BLK:3 * BLK], q0[c]) + dot_nn(w_row[here, 3 * BLK:], xl_in[c])
            send_r[c, here, :] = term.astype(BF16)
        t_right(c).start()

    @pl.loop(0, NC)
    def _(c):
        for h in range(HALVES):
            here = slice(h * HB, (h + 1) * HB)
            xl_in[c, here, :] = jnp.where(mask_of(far_r, (HB, CW)), xr_in[c, here, :], xl_in[c, here, :])
        add_scores(0, 0, c, q0, xl_in)

    tell_r.wait()
    tell_l.wait()
    end = far_l + far_r

    def pick(from_left, from_right, own):
        out = own
        if from_left is not None:
            out = jnp.where(mask_of(far_l, (1, BLK)), msg_l[0:1, from_left * BLK:(from_left + 1) * BLK], out)
        if from_right is not None:
            out = jnp.where(mask_of(far_r, (1, BLK)), msg_r[0:1, from_right * BLK:(from_right + 1) * BLK], out)
        return out

    own_cols = [col_lse[0:1, k * BLK:(k + 1) * BLK] for k in range(3)]
    lse_l = pick(1, None, own_cols[0])
    lse_0 = pick(2, 0, own_cols[1])
    lse_r = pick(None, 1, own_cols[2])
    lse_x = pick(0, 2, own_cols[0])
    pos_t[...] = jnp.broadcast_to(pos_ref[...].astype(F32), (128, BLK)).T
    flags = (has_l, jnp.int32(1), has_r, end)
    WT = 128

    @pl.loop(0, BLK // WT)
    def _(t):
        here = pl.ds(pl.multiple_of(t * WT, WT), WT)
        own = pl.ds(pl.multiple_of(BLK + t * WT, WT), WT)
        shape = (WT, BLK)
        raw = [s3[own, k * BLK:(k + 1) * BLK] * SCALE for k in range(3)] + [s3[here, :BLK] * SCALE]
        tiles = [jnp.where(mask_of(flag, shape), tile, LOWEST) for flag, tile in zip(flags, raw)]
        top = jnp.max(
            jnp.maximum(jnp.maximum(tiles[0], tiles[1]), jnp.maximum(tiles[2], tiles[3])), axis=1, keepdims=True
        )
        total = jnp.zeros((WT, 1), F32)
        for tile in tiles:
            total = total + jnp.sum(jnp.exp(tile - top), axis=1, keepdims=True)
        lse_rows = top + jnp.log(total)
        lane = lax.broadcasted_iota(jnp.int32, shape, 1).astype(F32)
        onehot = jnp.concatenate([pos_t[here, :]] * 4, axis=1) == lane
        hits = jnp.where(onehot, lse_0 - 2.0 * raw[1], 0.0)
        loss = lse_rows + jnp.sum(hits, axis=1, keepdims=True)
        loss_ref[:, here] = jnp.broadcast_to(loss, (WT, 128)).T[0:1, :]
        for k, (flag, tile, lse_cols) in enumerate(zip(flags, raw, (lse_l, lse_0, lse_r, lse_x))):
            value = weight_tile(tile, lse_rows, lse_cols)
            if k == 1:
                value = jnp.where(onehot, value - 2.0, value)
            value = jnp.where(mask_of(flag, shape), value, 0.0)
            w_row[here, k * BLK:(k + 1) * BLK] = value.astype(BF16)
            if k == 1:
                wt_p[:, here] = value.T.astype(BF16)

    weights_t(0, 1, wt_p, BLK)
    weights_t(2, 1, wt_p, 2 * BLK)

    def gq_out(c, slot):
        return pltpu.make_async_copy(stage.at[slot], gq_hbm.at[:, columns(c)], out_sem.at[slot])

    def gp_out(c, slot):
        return pltpu.make_async_copy(stage.at[slot], gp_hbm.at[:, columns(c)], out_sem.at[slot])

    @pl.loop(0, NC)
    def _(c):
        slot = lax.rem(c, 2)

        @pl.when(c >= 2)
        def _():
            gq_out(c - 2, slot).wait()

        for h in range(HALVES):
            here = slice(h * HB, (h + 1) * HB)
            total = dot_nn(w_row[here, :BLK], pl_in[c]) + dot_nn(w_row[here, BLK:2 * BLK], p0[c])
            total = total + dot_nn(w_row[here, 2 * BLK:3 * BLK], pr_in[c]) + dot_nn(w_row[here, 3 * BLK:], xl_in[c])
            stage[slot, here, :] = total.astype(BF16)
        gq_out(c, slot).start()

    @pl.loop(0, NC)
    def _(c):
        slot = lax.rem(c, 2)

        @pl.when(c < 2)
        def _():
            gq_out(NC - 2 + c, slot).wait()

        @pl.when(c >= 2)
        def _():
            gp_out(c - 2, slot).wait()

        t_right(c).wait_recv()
        t_left(c).wait_recv()
        shape = (HB, CW)
        for h in range(HALVES):
            here = slice(h * HB, (h + 1) * HB)
            total = dot_nn(wt_p[here, :BLK], q0[c]) + dot_nn(wt_p[here, BLK:2 * BLK], xl_in[c])
            total = total + dot_nn(wt_p[here, 2 * BLK:], xr_in[c])
            total = total + jnp.where(mask_of(far_l, shape), tl_in[c, here, :].astype(F32), 0.0)
            total = total + jnp.where(mask_of(far_r, shape), tr_in[c, here, :].astype(F32), 0.0)
            stage[slot, here, :] = total.astype(BF16)
        gp_out(c, slot).start()

    for c in (NC - 2, NC - 1):
        gp_out(c, c % 2).wait()

    @pl.loop(0, NC)
    def _(c):
        p_right(c).wait_send()
        p_left(c).wait_send()
        t_right(c).wait_send()
        t_left(c).wait_send()


def per_device(queries, passages, cluster_sizes, positives):
    block = pltpu.VMEM((NC, BLK, CW), BF16)
    dma = pltpu.SemaphoreType.DMA
    any_space = pl.BlockSpec(memory_space=pl.ANY)
    in_vmem = pl.BlockSpec(memory_space=pltpu.VMEM)
    return pl.pallas_call(
        exchange_kernel,
        out_shape=(
            jax.ShapeDtypeStruct((BLK, D), BF16),
            jax.ShapeDtypeStruct((BLK, D), BF16),
            jax.ShapeDtypeStruct((1, BLK), F32),
        ),
        in_specs=[pl.BlockSpec(memory_space=pltpu.SMEM), in_vmem, any_space, any_space],
        out_specs=(any_space, any_space, in_vmem),
        scratch_shapes=[block] * 10
        + [
            pltpu.VMEM((3 * BLK, 3 * BLK), F32),
            pltpu.VMEM((3 * BLK, 128), F32),
            pltpu.VMEM((8, 3 * BLK), F32),
            pltpu.VMEM((8, 3 * BLK), F32),
            pltpu.VMEM((8, 3 * BLK), F32),
            pltpu.VMEM((BLK, 128), F32),
            pltpu.VMEM((BLK, 4 * BLK), BF16),
            pltpu.VMEM((BLK, 3 * BLK), BF16),
            pltpu.VMEM((2, BLK, CW), BF16),
        ]
        + [dma((NC,))] * 14
        + [dma((2,))] * 3,
        compiler_params=pltpu.CompilerParams(
            collective_id=0, has_side_effects=True, vmem_limit_bytes=VM * 1024 * 1024
        ),
        cost_estimate=pl.CostEstimate(flops=50_000_000_000, bytes_accessed=64 << 20, transcendentals=0),
    )(cluster_sizes, positives, queries, passages)


def solution(mesh):
    placed = (P(("pb", "pa"), None), P(("pb", "pa"), None), P(), P(("pb", "pa"), None))
    return jax.shard_map(
        per_device,
        mesh=mesh,
        in_specs=placed,
        out_specs=(P(("pb", "pa"), None), P(("pb", "pa"), None), P(("pb", "pa"), None)),
        check_vma=False,
    )
```

```python
import jax
import jax.numpy as jnp
from jax import lax
from jax.experimental import pallas as pl
from jax.experimental.pallas import tpu as pltpu
from jax.sharding import PartitionSpec as P

BLK = 512
D = 4096
NB = 128
NCL = 64
NC = 8
CW = D // NC
PA = 16
HALVES = 2
HOLD = 6
VM = 62
HB = BLK // HALVES
LOWEST = -1e30
SCALE = float(D) ** (-0.5)
F32 = jnp.float32
BF16 = jnp.bfloat16
MESH = pl.DeviceIdType.MESH


def dot_nt(a, b):
    return lax.dot_general(a, b, (((1,), (1,)), ((), ())), preferred_element_type=F32)


def dot_nn(a, b):
    return jnp.dot(a, b, preferred_element_type=F32)


def mask_of(flag, shape):
    return jnp.full(shape, flag, jnp.int32) > 0


def exchange_kernel(
    sizes_ref, pos_ref, q_hbm, p_hbm,
    gq_hbm, gp_hbm, loss_ref,
    q0, p0, pl_in, pr_in, xl_in, xr_in, tl_in, tr_in, send_r, send_l,
    s3, row_lse, col_lse, msg_l, msg_r, pos_t, w_row, wt_p, stage,
    sem_q, sem_p, ps_r, ps_l, pr_r, pr_l, xs_r, xs_l, xr_r, xr_l, ts_r, ts_l, tr_r, tr_l,
    msg_send, msg_recv, out_sem, token,
):
    pb, pa = lax.axis_index("pb"), lax.axis_index("pa")
    me = pb * PA + pa
    after = lax.rem(me + 1, NB)
    before = lax.rem(me + NB - 1, NB)
    right = (after // PA, lax.rem(after, PA))
    left = (before // PA, lax.rem(before, PA))

    core = lax.rem(pb, 2)
    twin = (pb + 1 - 2 * core, pa)

    barrier = pltpu.get_barrier_semaphore()
    for neighbour in (left, right, twin):
        pl.semaphore_signal(barrier, inc=1, device_id=neighbour, device_id_type=MESH)
    pl.semaphore_wait(barrier, 3)

    WAYS = ("r", "l")
    order = {
        "r": lax.rem(core + jnp.where(pa == PA - 1, 1, 0), 2),
        "l": lax.rem(core + jnp.where(pa == 0, 1, 0), 2),
    }
    mixed = jnp.logical_or(pa == PA - 1, pa == 0)
    give_at = jnp.where(mixed, NC - HOLD, NC - 1)

    def columns(c):
        return pl.ds(pl.multiple_of(c * CW, CW), CW)

    def remote(src, dst, send, recv, to):
        return pltpu.make_async_remote_copy(
            src_ref=src, dst_ref=dst, send_sem=send, recv_sem=recv, device_id=to, device_id_type=MESH
        )

    def p_right(c):
        return remote(p_hbm.at[:, columns(c)], pl_in.at[c], ps_r.at[c], pr_r.at[c], right)

    def p_left(c):
        return remote(p_hbm.at[:, columns(c)], pr_in.at[c], ps_l.at[c], pr_l.at[c], left)

    def x_right(c):
        return remote(send_r.at[c], xl_in.at[c], xs_r.at[c], xr_r.at[c], right)

    def x_left(c):
        return remote(send_l.at[c], xr_in.at[c], xs_l.at[c], xr_l.at[c], left)

    def t_right(c):
        return remote(send_r.at[c], tl_in.at[c], ts_r.at[c], tr_r.at[c], right)

    def t_left(c):
        return remote(send_l.at[c], tr_in.at[c], ts_l.at[c], tr_l.at[c], left)

    def q_load(c):
        return pltpu.make_async_copy(q_hbm.at[:, columns(c)], q0.at[c], sem_q.at[c])

    def p_load(c):
        return pltpu.make_async_copy(p_hbm.at[:, columns(c)], p0.at[c], sem_p.at[c])

    @pl.loop(0, NC)
    def _(c):
        p_right(c).start()
        p_left(c).start()
        q_load(c).start()
        p_load(c).start()

    def scan_sizes(k, carry):
        end, at_me, at_next, at_before, at_after = carry
        end = end + sizes_ref[k]
        one = jnp.int32(1)
        return (
            end,
            jnp.where(end == me, one, at_me),
            jnp.where(end == me + 1, one, at_next),
            jnp.where(end == me - 1, one, at_before),
            jnp.where(end == me + 2, one, at_after),
        )

    zero = jnp.int32(0)
    _, at_me, at_next, at_before, at_after = lax.fori_loop(0, NCL, scan_sizes, (zero,) * 5)
    has_l = jnp.where(me > 0, 1 - at_me, 0)
    has_r = jnp.where(me < NB - 1, 1 - at_next, 0)
    far_l = jnp.where(me > 1, 1 - at_before, 0) * has_l
    far_r = jnp.where(me < NB - 2, 1 - at_after, 0) * has_r
    rows_l = has_l - far_l
    rows_r = has_r - far_r

    def add_scores(r, k, c, a_ref, b_ref):
        for h in range(HALVES):
            ref = s3.at[pl.ds(r * BLK + h * HB, HB), pl.ds(k * BLK, BLK)]
            part = dot_nt(a_ref[c, h * HB:(h + 1) * HB, :], b_ref[c])

            @pl.when(c == 0)
            def _():
                ref[...] = part

            @pl.when(c > 0)
            def _():
                ref[...] += part

    @pl.loop(0, NC)
    def _(c):
        q_load(c).wait()
        p_load(c).wait()
        add_scores(1, 1, c, q0, p0)

    @pl.loop(0, NC)
    def _(c):
        p_right(c).wait_recv()
        p_left(c).wait_recv()
        for h in range(HALVES):
            here = slice(h * HB, (h + 1) * HB)
            send_r[c, here, :] = jnp.where(mask_of(has_l, (HB, CW)), pl_in[c, here, :], q0[c, here, :])
        @pl.when(jnp.logical_or(order["r"] == 0, c < NC - HOLD))
        def _():
            x_right(c).start()

        for h in range(HALVES):
            here = slice(h * HB, (h + 1) * HB)
            send_l[c, here, :] = jnp.where(mask_of(has_r, (HB, CW)), pr_in[c, here, :], q0[c, here, :])
        @pl.when(jnp.logical_or(order["l"] == 0, c < NC - HOLD))
        def _():
            x_left(c).start()

        add_scores(1, 0, c, q0, pl_in)
        add_scores(1, 2, c, q0, pr_in)

    send_x = {"r": x_right, "l": x_left}

    @pl.loop(0, NC)
    def _(c):
        for at, way in enumerate(WAYS):
            @pl.when(jnp.logical_and(c == give_at, order[way] == 0))
            def _():
                @pl.loop(0, NC - 1)
                def _(k):
                    send_x[way](k).wait_send()

                pl.semaphore_signal(token.at[at], inc=1, device_id=twin, device_id_type=MESH)

        for at, way in enumerate(WAYS):
            @pl.when(jnp.logical_and(c == NC - HOLD, order[way] == 1))
            def _():
                pl.semaphore_wait(token.at[at], 1)

                @pl.loop(NC - HOLD, NC)
                def _(k):
                    send_x[way](k).start()

        x_right(c).wait_recv()
        x_left(c).wait_recv()
        for r, x_in in ((0, xl_in), (2, xr_in)):
            for k, p_in in ((0, pl_in), (1, p0), (2, pr_in)):
                add_scores(r, k, c, x_in, p_in)

    held_rows = (rows_l, jnp.int32(1), rows_r)
    held_cols = (has_l, jnp.int32(1), has_r)
    RT = 64

    def valid(r, k, shape):
        return mask_of(held_rows[r] * held_cols[k], shape)

    col_peak = [jnp.full((8, BLK), LOWEST, F32) for _ in range(3)]
    for r in range(3):
        def peaks(t, peak):
            rows = pl.ds(pl.multiple_of(r * BLK + t * RT, RT), RT)
            tiles = [
                jnp.where(valid(r, k, (RT, BLK)), s3[rows, k * BLK:(k + 1) * BLK] * SCALE, LOWEST)
                for k in range(3)
            ]
            top = jnp.max(jnp.maximum(jnp.maximum(tiles[0], tiles[1]), tiles[2]), axis=1, keepdims=True)
            total = jnp.zeros((RT, 1), F32)
            for tile in tiles:
                total = total + jnp.sum(jnp.exp(tile - top), axis=1, keepdims=True)
            row_lse[rows, :] = jnp.broadcast_to(top + jnp.log(total), (RT, 128))
            return tuple(
                jnp.maximum(old, jnp.max(tile.reshape(RT // 8, 8, BLK), axis=0))
                for old, tile in zip(peak, tiles)
            )

        col_peak = lax.fori_loop(0, BLK // RT, peaks, tuple(col_peak))
    col_top = [jnp.max(peak, axis=0, keepdims=True) for peak in col_peak]
    col_sum = [jnp.zeros((8, BLK), F32) for _ in range(3)]
    for r in range(3):
        def sums(t, total):
            rows = pl.ds(pl.multiple_of(r * BLK + t * RT, RT), RT)
            out = []
            for k in range(3):
                tile = jnp.where(valid(r, k, (RT, BLK)), s3[rows, k * BLK:(k + 1) * BLK] * SCALE, LOWEST)
                part = jnp.exp(tile - col_top[k])
                out.append(total[k] + jnp.sum(part.reshape(RT // 8, 8, BLK), axis=0))
            return tuple(out)

        col_sum = lax.fori_loop(0, BLK // RT, sums, tuple(col_sum))
    for k in range(3):
        lse = col_top[k] + jnp.log(jnp.sum(col_sum[k], axis=0, keepdims=True))
        col_lse[:, k * BLK:(k + 1) * BLK] = jnp.broadcast_to(lse, (8, BLK))

    tell_r = remote(col_lse, msg_l, msg_send.at[0], msg_recv.at[0], right)
    tell_l = remote(col_lse, msg_r, msg_send.at[1], msg_recv.at[1], left)
    tell_r.start()
    tell_l.start()

    def weight_tile(tile, lse_rows, lse_cols):
        return jnp.exp(tile - lse_rows) + jnp.exp(tile - lse_cols)

    def weights_t(r, k, out, at):
        ok = held_rows[r] * held_cols[k]
        lse_cols = col_lse[0:1, k * BLK:(k + 1) * BLK]

        @pl.loop(0, 4)
        def _(t):
            rows = pl.ds(pl.multiple_of(r * BLK + t * 128, 128), 128)
            tile = s3[rows, k * BLK:(k + 1) * BLK] * SCALE
            value = weight_tile(tile, row_lse[rows, 0:1], lse_cols)
            value = jnp.where(mask_of(ok, value.shape), value, 0.0)
            out[:, pl.ds(pl.multiple_of(at + t * 128, 128), 128)] = value.T.astype(BF16)

    for place, (r, k) in enumerate(((1, 0), (2, 0), (1, 2), (0, 2))):
        weights_t(r, k, w_row, place * BLK)

    @pl.loop(0, NC)
    def _(c):
        @pl.when(jnp.logical_or(order["l"] == 1, c == NC - 1))
        def _():
            x_left(c).wait_send()

        for h in range(HALVES):
            here = slice(h * HB, (h + 1) * HB)
            term = dot_nn(w_row[here, :BLK], q0[c]) + dot_nn(w_row[here, BLK:2 * BLK], xr_in[c])
            send_l[c, here, :] = term.astype(BF16)
        t_left(c).start()
        @pl.when(jnp.logical_or(order["r"] == 1, c == NC - 1))
        def _():
            x_right(c).wait_send()

        for h in range(HALVES):
            here = slice(h * HB, (h + 1) * HB)
            term = dot_nn(w_row[here, 2 * BLK:3 * BLK], q0[c]) + dot_nn(w_row[here, 3 * BLK:], xl_in[c])
            send_r[c, here, :] = term.astype(BF16)
        t_right(c).start()

    @pl.loop(0, NC)
    def _(c):
        for h in range(HALVES):
            here = slice(h * HB, (h + 1) * HB)
            xl_in[c, here, :] = jnp.where(mask_of(far_r, (HB, CW)), xr_in[c, here, :], xl_in[c, here, :])
        add_scores(0, 0, c, q0, xl_in)

    tell_r.wait()
    tell_l.wait()
    end = far_l + far_r

    def pick(from_left, from_right, own):
        out = own
        if from_left is not None:
            out = jnp.where(mask_of(far_l, (1, BLK)), msg_l[0:1, from_left * BLK:(from_left + 1) * BLK], out)
        if from_right is not None:
            out = jnp.where(mask_of(far_r, (1, BLK)), msg_r[0:1, from_right * BLK:(from_right + 1) * BLK], out)
        return out

    own_cols = [col_lse[0:1, k * BLK:(k + 1) * BLK] for k in range(3)]
    lse_l = pick(1, None, own_cols[0])
    lse_0 = pick(2, 0, own_cols[1])
    lse_r = pick(None, 1, own_cols[2])
    lse_x = pick(0, 2, own_cols[0])
    pos_t[...] = jnp.broadcast_to(pos_ref[...].astype(F32), (128, BLK)).T
    flags = (has_l, jnp.int32(1), has_r, end)
    WT = 128

    @pl.loop(0, BLK // WT)
    def _(t):
        here = pl.ds(pl.multiple_of(t * WT, WT), WT)
        own = pl.ds(pl.multiple_of(BLK + t * WT, WT), WT)
        shape = (WT, BLK)
        raw = [s3[own, k * BLK:(k + 1) * BLK] * SCALE for k in range(3)] + [s3[here, :BLK] * SCALE]
        tiles = [jnp.where(mask_of(flag, shape), tile, LOWEST) for flag, tile in zip(flags, raw)]
        top = jnp.max(
            jnp.maximum(jnp.maximum(tiles[0], tiles[1]), jnp.maximum(tiles[2], tiles[3])), axis=1, keepdims=True
        )
        total = jnp.zeros((WT, 1), F32)
        for tile in tiles:
            total = total + jnp.sum(jnp.exp(tile - top), axis=1, keepdims=True)
        lse_rows = top + jnp.log(total)
        lane = lax.broadcasted_iota(jnp.int32, shape, 1).astype(F32)
        onehot = jnp.concatenate([pos_t[here, :]] * 4, axis=1) == lane
        hits = jnp.where(onehot, lse_0 - 2.0 * raw[1], 0.0)
        loss = lse_rows + jnp.sum(hits, axis=1, keepdims=True)
        loss_ref[:, here] = jnp.broadcast_to(loss, (WT, 128)).T[0:1, :]
        for k, (flag, tile, lse_cols) in enumerate(zip(flags, raw, (lse_l, lse_0, lse_r, lse_x))):
            value = weight_tile(tile, lse_rows, lse_cols)
            if k == 1:
                value = jnp.where(onehot, value - 2.0, value)
            value = jnp.where(mask_of(flag, shape), value, 0.0)
            w_row[here, k * BLK:(k + 1) * BLK] = value.astype(BF16)
            if k == 1:
                wt_p[:, here] = value.T.astype(BF16)

    weights_t(0, 1, wt_p, BLK)
    weights_t(2, 1, wt_p, 2 * BLK)

    def gq_out(c, slot):
        return pltpu.make_async_copy(stage.at[slot], gq_hbm.at[:, columns(c)], out_sem.at[slot])

    def gp_out(c, slot):
        return pltpu.make_async_copy(stage.at[slot], gp_hbm.at[:, columns(c)], out_sem.at[slot])

    @pl.loop(0, NC)
    def _(c):
        slot = lax.rem(c, 2)

        @pl.when(c >= 2)
        def _():
            gq_out(c - 2, slot).wait()

        for h in range(HALVES):
            here = slice(h * HB, (h + 1) * HB)
            total = dot_nn(w_row[here, :BLK], pl_in[c]) + dot_nn(w_row[here, BLK:2 * BLK], p0[c])
            total = total + dot_nn(w_row[here, 2 * BLK:3 * BLK], pr_in[c]) + dot_nn(w_row[here, 3 * BLK:], xl_in[c])
            stage[slot, here, :] = total.astype(BF16)
        gq_out(c, slot).start()

    @pl.loop(0, NC)
    def _(c):
        slot = lax.rem(c, 2)

        @pl.when(c < 2)
        def _():
            gq_out(NC - 2 + c, slot).wait()

        @pl.when(c >= 2)
        def _():
            gp_out(c - 2, slot).wait()

        t_right(c).wait_recv()
        t_left(c).wait_recv()
        shape = (HB, CW)
        for h in range(HALVES):
            here = slice(h * HB, (h + 1) * HB)
            total = dot_nn(wt_p[here, :BLK], q0[c]) + dot_nn(wt_p[here, BLK:2 * BLK], xl_in[c])
            total = total + dot_nn(wt_p[here, 2 * BLK:], xr_in[c])
            total = total + jnp.where(mask_of(far_l, shape), tl_in[c, here, :].astype(F32), 0.0)
            total = total + jnp.where(mask_of(far_r, shape), tr_in[c, here, :].astype(F32), 0.0)
            stage[slot, here, :] = total.astype(BF16)
        gp_out(c, slot).start()

    for c in (NC - 2, NC - 1):
        gp_out(c, c % 2).wait()

    @pl.loop(0, NC)
    def _(c):
        p_right(c).wait_send()
        p_left(c).wait_send()
        t_right(c).wait_send()
        t_left(c).wait_send()


def per_device(queries, passages, cluster_sizes, positives):
    block = pltpu.VMEM((NC, BLK, CW), BF16)
    dma = pltpu.SemaphoreType.DMA
    any_space = pl.BlockSpec(memory_space=pl.ANY)
    in_vmem = pl.BlockSpec(memory_space=pltpu.VMEM)
    return pl.pallas_call(
        exchange_kernel,
        out_shape=(
            jax.ShapeDtypeStruct((BLK, D), BF16),
            jax.ShapeDtypeStruct((BLK, D), BF16),
            jax.ShapeDtypeStruct((1, BLK), F32),
        ),
        in_specs=[pl.BlockSpec(memory_space=pltpu.SMEM), in_vmem, any_space, any_space],
        out_specs=(any_space, any_space, in_vmem),
        scratch_shapes=[block] * 10
        + [
            pltpu.VMEM((3 * BLK, 3 * BLK), F32),
            pltpu.VMEM((3 * BLK, 128), F32),
            pltpu.VMEM((8, 3 * BLK), F32),
            pltpu.VMEM((8, 3 * BLK), F32),
            pltpu.VMEM((8, 3 * BLK), F32),
            pltpu.VMEM((BLK, 128), F32),
            pltpu.VMEM((BLK, 4 * BLK), BF16),
            pltpu.VMEM((BLK, 3 * BLK), BF16),
            pltpu.VMEM((2, BLK, CW), BF16),
        ]
        + [dma((NC,))] * 14
        + [dma((2,))] * 3
        + [pltpu.SemaphoreType.REGULAR((2,))],
        compiler_params=pltpu.CompilerParams(
            collective_id=0, has_side_effects=True, vmem_limit_bytes=VM * 1024 * 1024
        ),
        cost_estimate=pl.CostEstimate(flops=50_000_000_000, bytes_accessed=64 << 20, transcendentals=0),
    )(cluster_sizes, positives, queries, passages)


def solution(mesh):
    placed = (P(("pb", "pa"), None), P(("pb", "pa"), None), P(), P(("pb", "pa"), None))
    return jax.shard_map(
        per_device,
        mesh=mesh,
        in_specs=placed,
        out_specs=(P(("pb", "pa"), None), P(("pb", "pa"), None), P(("pb", "pa"), None)),
        check_vma=False,
    )
```

```python
import jax
import jax.numpy as jnp
from jax import lax
from jax.experimental import pallas as pl
from jax.experimental.pallas import tpu as pltpu
from jax.sharding import PartitionSpec as P

BLK = 512
D = 4096
NB = 128
NCL = 64
NC = 8
CW = D // NC
PA = 16
HALVES = 2
HOLD = 6
VM = 62
HB = BLK // HALVES
LOWEST = -1e30
SCALE = float(D) ** (-0.5)
F32 = jnp.float32
BF16 = jnp.bfloat16
MESH = pl.DeviceIdType.MESH


def dot_nt(a, b):
    return lax.dot_general(a, b, (((1,), (1,)), ((), ())), preferred_element_type=F32)


def dot_nn(a, b):
    return jnp.dot(a, b, preferred_element_type=F32)


def mask_of(flag, shape):
    return jnp.full(shape, flag, jnp.int32) > 0


def exchange_kernel(
    sizes_ref, pos_ref, q_hbm, p_hbm,
    gq_hbm, gp_hbm, loss_ref,
    q0, p0, pl_in, pr_in, xl_in, xr_in, tl_in, tr_in, send_r, send_l,
    s3, row_lse, col_peak, col_sum, col_lse, msg_l, msg_r, pos_t, w_row, wt_p, stage,
    sem_q, sem_p, ps_r, ps_l, pr_r, pr_l, xs_r, xs_l, xr_r, xr_l, ts_r, ts_l, tr_r, tr_l,
    msg_send, msg_recv, out_sem, token,
):
    pb, pa = lax.axis_index("pb"), lax.axis_index("pa")
    me = pb * PA + pa
    after = lax.rem(me + 1, NB)
    before = lax.rem(me + NB - 1, NB)
    right = (after // PA, lax.rem(after, PA))
    left = (before // PA, lax.rem(before, PA))

    core = lax.rem(pb, 2)
    twin = (pb + 1 - 2 * core, pa)

    barrier = pltpu.get_barrier_semaphore()
    for neighbour in (left, right, twin):
        pl.semaphore_signal(barrier, inc=1, device_id=neighbour, device_id_type=MESH)
    pl.semaphore_wait(barrier, 3)

    WAYS = ("r", "l")
    order = {
        "r": lax.rem(core + jnp.where(pa == PA - 1, 1, 0), 2),
        "l": lax.rem(core + jnp.where(pa == 0, 1, 0), 2),
    }
    mixed = jnp.logical_or(pa == PA - 1, pa == 0)
    give_at = jnp.where(mixed, NC - HOLD, NC - 1)

    def columns(c):
        return pl.ds(pl.multiple_of(c * CW, CW), CW)

    def remote(src, dst, send, recv, to):
        return pltpu.make_async_remote_copy(
            src_ref=src, dst_ref=dst, send_sem=send, recv_sem=recv, device_id=to, device_id_type=MESH
        )

    def p_right(c):
        return remote(p_hbm.at[:, columns(c)], pl_in.at[c], ps_r.at[c], pr_r.at[c], right)

    def p_left(c):
        return remote(p_hbm.at[:, columns(c)], pr_in.at[c], ps_l.at[c], pr_l.at[c], left)

    def x_right(c):
        return remote(send_r.at[c], xl_in.at[c], xs_r.at[c], xr_r.at[c], right)

    def x_left(c):
        return remote(send_l.at[c], xr_in.at[c], xs_l.at[c], xr_l.at[c], left)

    def t_right(c):
        return remote(send_r.at[c], tl_in.at[c], ts_r.at[c], tr_r.at[c], right)

    def t_left(c):
        return remote(send_l.at[c], tr_in.at[c], ts_l.at[c], tr_l.at[c], left)

    def q_load(c):
        return pltpu.make_async_copy(q_hbm.at[:, columns(c)], q0.at[c], sem_q.at[c])

    def p_load(c):
        return pltpu.make_async_copy(p_hbm.at[:, columns(c)], p0.at[c], sem_p.at[c])

    @pl.loop(0, NC)
    def _(c):
        p_right(c).start()
        p_left(c).start()
        q_load(c).start()
        p_load(c).start()

    def scan_sizes(k, carry):
        end, at_me, at_next, at_before, at_after = carry
        end = end + sizes_ref[k]
        one = jnp.int32(1)
        return (
            end,
            jnp.where(end == me, one, at_me),
            jnp.where(end == me + 1, one, at_next),
            jnp.where(end == me - 1, one, at_before),
            jnp.where(end == me + 2, one, at_after),
        )

    zero = jnp.int32(0)
    _, at_me, at_next, at_before, at_after = lax.fori_loop(0, NCL, scan_sizes, (zero,) * 5)
    has_l = jnp.where(me > 0, 1 - at_me, 0)
    has_r = jnp.where(me < NB - 1, 1 - at_next, 0)
    far_l = jnp.where(me > 1, 1 - at_before, 0) * has_l
    far_r = jnp.where(me < NB - 2, 1 - at_after, 0) * has_r
    rows_l = has_l - far_l
    rows_r = has_r - far_r
    end = far_l + far_r

    def add_scores(r, k, c, a_ref, b_ref, held):
        for h in range(HALVES):
            ref = s3.at[pl.ds(r * BLK + h * HB, HB), pl.ds(k * BLK, BLK)]
            part = dot_nt(a_ref[c, h * HB:(h + 1) * HB, :], b_ref[c])

            @pl.when(c == 0)
            def _():
                ref[...] = part

            @pl.when(jnp.logical_and(c > 0, c < NC - 1))
            def _():
                ref[...] += part

            @pl.when(c == NC - 1)
            def _():
                ref[...] = jnp.where(mask_of(held, (HB, BLK)), (ref[...] + part) * SCALE, LOWEST)

    held_rows = (rows_l, jnp.int32(1), rows_r)
    held_cols = (has_l, jnp.int32(1), has_r)
    RT = 64

    def block_row_stats(r):
        def step(t, carry):
            rows = pl.ds(pl.multiple_of(r * BLK + t * RT, RT), RT)
            top = jnp.full((RT, 128), LOWEST, F32)
            for k in range(12):
                top = jnp.maximum(top, s3[rows, k * 128:(k + 1) * 128])
            top = jnp.max(top, axis=1, keepdims=True)
            total = jnp.zeros((RT, 128), F32)
            out = []
            for k in range(3):
                tile = s3[rows, k * BLK:(k + 1) * BLK]
                part = jnp.exp(tile - top)
                for j in range(4):
                    total = total + part[:, j * 128:(j + 1) * 128]
                old_peak, old_sum = carry[2 * k], carry[2 * k + 1]
                split = tile.reshape(RT // 8, 8, BLK)
                peak = jnp.maximum(old_peak, jnp.max(split, axis=0))
                out.append(peak)
                out.append(old_sum * jnp.exp(old_peak - peak) + jnp.sum(jnp.exp(split - peak[None]), axis=0))
            lse = top + jnp.log(jnp.sum(total, axis=1, keepdims=True))
            row_lse[rows, :] = jnp.broadcast_to(lse, (RT, 128))
            return tuple(out)

        carry = []
        for k in range(3):
            carry += [col_peak[:, k * BLK:(k + 1) * BLK], col_sum[:, k * BLK:(k + 1) * BLK]]
        carry = lax.fori_loop(0, BLK // RT, step, tuple(carry))
        for k in range(3):
            col_peak[:, k * BLK:(k + 1) * BLK] = carry[2 * k]
            col_sum[:, k * BLK:(k + 1) * BLK] = carry[2 * k + 1]

    col_peak[...] = jnp.full((8, 3 * BLK), LOWEST, F32)
    col_sum[...] = jnp.zeros((8, 3 * BLK), F32)

    @pl.loop(0, NC)
    def _(c):
        q_load(c).wait()
        p_load(c).wait()
        add_scores(1, 1, c, q0, p0, jnp.int32(1))

    @pl.loop(0, NC)
    def _(c):
        p_right(c).wait_recv()
        p_left(c).wait_recv()
        for h in range(HALVES):
            here = slice(h * HB, (h + 1) * HB)
            send_r[c, here, :] = jnp.where(mask_of(has_l, (HB, CW)), pl_in[c, here, :], q0[c, here, :])
        @pl.when(jnp.logical_or(order["r"] == 0, c < NC - HOLD))
        def _():
            x_right(c).start()

        for h in range(HALVES):
            here = slice(h * HB, (h + 1) * HB)
            send_l[c, here, :] = jnp.where(mask_of(has_r, (HB, CW)), pr_in[c, here, :], q0[c, here, :])
        @pl.when(jnp.logical_or(order["l"] == 0, c < NC - HOLD))
        def _():
            x_left(c).start()

        add_scores(1, 0, c, q0, pl_in, has_l)
        add_scores(1, 2, c, q0, pr_in, has_r)

    send_x = {"r": x_right, "l": x_left}
    block_row_stats(1)

    @pl.loop(0, NC)
    def _(c):
        for at, way in enumerate(WAYS):
            @pl.when(jnp.logical_and(c == give_at, order[way] == 0))
            def _():
                @pl.loop(0, NC - 1)
                def _(k):
                    send_x[way](k).wait_send()

                pl.semaphore_signal(token.at[at], inc=1, device_id=twin, device_id_type=MESH)

        for at, way in enumerate(WAYS):
            @pl.when(jnp.logical_and(c == NC - HOLD, order[way] == 1))
            def _():
                pl.semaphore_wait(token.at[at], 1)

                @pl.loop(NC - HOLD, NC)
                def _(k):
                    send_x[way](k).start()

        x_right(c).wait_recv()
        x_left(c).wait_recv()
        for r, x_in in ((0, xl_in), (2, xr_in)):
            for k, p_in in ((0, pl_in), (1, p0), (2, pr_in)):
                add_scores(r, k, c, x_in, p_in, held_rows[r] * held_cols[k])

    block_row_stats(0)
    block_row_stats(2)
    for k in range(3):
        here = slice(k * BLK, (k + 1) * BLK)
        peak = jnp.max(col_peak[:, here], axis=0, keepdims=True)
        total = jnp.sum(col_sum[:, here] * jnp.exp(col_peak[:, here] - peak), axis=0, keepdims=True)
        col_lse[:, here] = jnp.broadcast_to(peak + jnp.log(total), (8, BLK))

    tell_r = remote(col_lse, msg_l, msg_send.at[0], msg_recv.at[0], right)
    tell_l = remote(col_lse, msg_r, msg_send.at[1], msg_recv.at[1], left)
    tell_r.start()
    tell_l.start()

    def weight_tile(tile, lse_rows, lse_cols):
        return jnp.exp(tile - lse_rows) + jnp.exp(tile - lse_cols)

    def weights_t(r, k, out, at):
        ok = held_rows[r] * held_cols[k]
        lse_cols = col_lse[0:1, k * BLK:(k + 1) * BLK]

        @pl.loop(0, 4)
        def _(t):
            rows = pl.ds(pl.multiple_of(r * BLK + t * 128, 128), 128)
            tile = s3[rows, k * BLK:(k + 1) * BLK]
            value = weight_tile(tile, row_lse[rows, 0:1], lse_cols)
            value = jnp.where(mask_of(ok, value.shape), value, 0.0)
            out[:, pl.ds(pl.multiple_of(at + t * 128, 128), 128)] = value.T.astype(BF16)

    for place, (r, k) in enumerate(((1, 0), (2, 0), (1, 2), (0, 2))):
        weights_t(r, k, w_row, place * BLK)

    @pl.loop(0, NC)
    def _(c):
        @pl.when(jnp.logical_or(order["l"] == 1, c == NC - 1))
        def _():
            x_left(c).wait_send()

        for h in range(HALVES):
            here = slice(h * HB, (h + 1) * HB)
            term = dot_nn(w_row[here, :BLK], q0[c]) + dot_nn(w_row[here, BLK:2 * BLK], xr_in[c])
            send_l[c, here, :] = term.astype(BF16)
        t_left(c).start()
        @pl.when(jnp.logical_or(order["r"] == 1, c == NC - 1))
        def _():
            x_right(c).wait_send()

        for h in range(HALVES):
            here = slice(h * HB, (h + 1) * HB)
            term = dot_nn(w_row[here, 2 * BLK:3 * BLK], q0[c]) + dot_nn(w_row[here, 3 * BLK:], xl_in[c])
            send_r[c, here, :] = term.astype(BF16)
        t_right(c).start()

    @pl.loop(0, NC)
    def _(c):
        for h in range(HALVES):
            here = slice(h * HB, (h + 1) * HB)
            xl_in[c, here, :] = jnp.where(mask_of(far_r, (HB, CW)), xr_in[c, here, :], xl_in[c, here, :])
        add_scores(0, 0, c, q0, xl_in, end)

    tell_r.wait()
    tell_l.wait()

    def pick(from_left, from_right, own):
        out = own
        if from_left is not None:
            out = jnp.where(mask_of(far_l, (1, BLK)), msg_l[0:1, from_left * BLK:(from_left + 1) * BLK], out)
        if from_right is not None:
            out = jnp.where(mask_of(far_r, (1, BLK)), msg_r[0:1, from_right * BLK:(from_right + 1) * BLK], out)
        return out

    own_cols = [col_lse[0:1, k * BLK:(k + 1) * BLK] for k in range(3)]
    lse_l = pick(1, None, own_cols[0])
    lse_0 = pick(2, 0, own_cols[1])
    lse_r = pick(None, 1, own_cols[2])
    lse_x = pick(0, 2, own_cols[0])
    pos_t[...] = jnp.broadcast_to(pos_ref[...].astype(F32), (128, BLK)).T
    flags = (has_l, jnp.int32(1), has_r, end)
    WT = 128

    @pl.loop(0, BLK // WT)
    def _(t):
        here = pl.ds(pl.multiple_of(t * WT, WT), WT)
        own = pl.ds(pl.multiple_of(BLK + t * WT, WT), WT)
        shape = (WT, BLK)
        tiles = [s3[own, k * BLK:(k + 1) * BLK] for k in range(3)] + [s3[here, :BLK]]
        top = jnp.max(
            jnp.maximum(jnp.maximum(tiles[0], tiles[1]), jnp.maximum(tiles[2], tiles[3])), axis=1, keepdims=True
        )
        total = jnp.zeros((WT, 1), F32)
        for tile in tiles:
            total = total + jnp.sum(jnp.exp(tile - top), axis=1, keepdims=True)
        lse_rows = top + jnp.log(total)
        lane = lax.broadcasted_iota(jnp.int32, shape, 1).astype(F32)
        onehot = jnp.concatenate([pos_t[here, :]] * 4, axis=1) == lane
        hits = jnp.where(onehot, lse_0 - 2.0 * tiles[1], 0.0)
        loss = lse_rows + jnp.sum(hits, axis=1, keepdims=True)
        loss_ref[:, here] = jnp.broadcast_to(loss, (WT, 128)).T[0:1, :]
        for k, (flag, tile, lse_cols) in enumerate(zip(flags, tiles, (lse_l, lse_0, lse_r, lse_x))):
            value = weight_tile(tile, lse_rows, lse_cols)
            if k == 1:
                value = jnp.where(onehot, value - 2.0, value)
            value = jnp.where(mask_of(flag, shape), value, 0.0)
            w_row[here, k * BLK:(k + 1) * BLK] = value.astype(BF16)
            if k == 1:
                wt_p[:, here] = value.T.astype(BF16)

    weights_t(0, 1, wt_p, BLK)
    weights_t(2, 1, wt_p, 2 * BLK)

    def gq_out(c, slot):
        return pltpu.make_async_copy(stage.at[slot], gq_hbm.at[:, columns(c)], out_sem.at[slot])

    def gp_out(c, slot):
        return pltpu.make_async_copy(stage.at[slot], gp_hbm.at[:, columns(c)], out_sem.at[slot])

    @pl.loop(0, NC)
    def _(c):
        slot = lax.rem(c, 2)

        @pl.when(c >= 2)
        def _():
            gq_out(c - 2, slot).wait()

        for h in range(HALVES):
            here = slice(h * HB, (h + 1) * HB)
            total = dot_nn(w_row[here, :BLK], pl_in[c]) + dot_nn(w_row[here, BLK:2 * BLK], p0[c])
            total = total + dot_nn(w_row[here, 2 * BLK:3 * BLK], pr_in[c]) + dot_nn(w_row[here, 3 * BLK:], xl_in[c])
            stage[slot, here, :] = total.astype(BF16)
        gq_out(c, slot).start()

    @pl.loop(0, NC)
    def _(c):
        slot = lax.rem(c, 2)

        @pl.when(c < 2)
        def _():
            gq_out(NC - 2 + c, slot).wait()

        @pl.when(c >= 2)
        def _():
            gp_out(c - 2, slot).wait()

        t_right(c).wait_recv()
        t_left(c).wait_recv()
        shape = (HB, CW)
        for h in range(HALVES):
            here = slice(h * HB, (h + 1) * HB)
            total = dot_nn(wt_p[here, :BLK], q0[c]) + dot_nn(wt_p[here, BLK:2 * BLK], xl_in[c])
            total = total + dot_nn(wt_p[here, 2 * BLK:], xr_in[c])
            total = total + jnp.where(mask_of(far_l, shape), tl_in[c, here, :].astype(F32), 0.0)
            total = total + jnp.where(mask_of(far_r, shape), tr_in[c, here, :].astype(F32), 0.0)
            stage[slot, here, :] = total.astype(BF16)
        gp_out(c, slot).start()

    for c in (NC - 2, NC - 1):
        gp_out(c, c % 2).wait()

    @pl.loop(0, NC)
    def _(c):
        p_right(c).wait_send()
        p_left(c).wait_send()
        t_right(c).wait_send()
        t_left(c).wait_send()


def per_device(queries, passages, cluster_sizes, positives):
    block = pltpu.VMEM((NC, BLK, CW), BF16)
    dma = pltpu.SemaphoreType.DMA
    any_space = pl.BlockSpec(memory_space=pl.ANY)
    in_vmem = pl.BlockSpec(memory_space=pltpu.VMEM)
    return pl.pallas_call(
        exchange_kernel,
        out_shape=(
            jax.ShapeDtypeStruct((BLK, D), BF16),
            jax.ShapeDtypeStruct((BLK, D), BF16),
            jax.ShapeDtypeStruct((1, BLK), F32),
        ),
        in_specs=[pl.BlockSpec(memory_space=pltpu.SMEM), in_vmem, any_space, any_space],
        out_specs=(any_space, any_space, in_vmem),
        scratch_shapes=[block] * 10
        + [
            pltpu.VMEM((3 * BLK, 3 * BLK), F32),
            pltpu.VMEM((3 * BLK, 128), F32),
            pltpu.VMEM((8, 3 * BLK), F32),
            pltpu.VMEM((8, 3 * BLK), F32),
            pltpu.VMEM((8, 3 * BLK), F32),
            pltpu.VMEM((8, 3 * BLK), F32),
            pltpu.VMEM((8, 3 * BLK), F32),
            pltpu.VMEM((BLK, 128), F32),
            pltpu.VMEM((BLK, 4 * BLK), BF16),
            pltpu.VMEM((BLK, 3 * BLK), BF16),
            pltpu.VMEM((2, BLK, CW), BF16),
        ]
        + [dma((NC,))] * 14
        + [dma((2,))] * 3
        + [pltpu.SemaphoreType.REGULAR((2,))],
        compiler_params=pltpu.CompilerParams(
            collective_id=0, has_side_effects=True, vmem_limit_bytes=VM * 1024 * 1024
        ),
        cost_estimate=pl.CostEstimate(flops=50_000_000_000, bytes_accessed=64 << 20, transcendentals=0),
    )(cluster_sizes, positives, queries, passages)


def solution(mesh):
    placed = (P(("pb", "pa"), None), P(("pb", "pa"), None), P(), P(("pb", "pa"), None))
    return jax.shard_map(
        per_device,
        mesh=mesh,
        in_specs=placed,
        out_specs=(P(("pb", "pa"), None), P(("pb", "pa"), None), P(("pb", "pa"), None)),
        check_vma=False,
    )
```

```python
import jax
import jax.numpy as jnp
from jax import lax
from jax.experimental import pallas as pl
from jax.experimental.pallas import tpu as pltpu
from jax.sharding import PartitionSpec as P

BLK = 512
D = 4096
NB = 128
NCL = 64
NC = 8
CW = D // NC
PA = 16
HALVES = 2
HOLD = 6
VM = 62
HB = BLK // HALVES
LOWEST = -1e30
SCALE = float(D) ** (-0.5)
F32 = jnp.float32
BF16 = jnp.bfloat16
MESH = pl.DeviceIdType.MESH


def dot_nt(a, b):
    return lax.dot_general(a, b, (((1,), (1,)), ((), ())), preferred_element_type=F32)


def dot_nn(a, b):
    return jnp.dot(a, b, preferred_element_type=F32)


def mask_of(flag, shape):
    return jnp.full(shape, flag, jnp.int32) > 0


def exchange_kernel(
    sizes_ref, pos_ref, q_hbm, p_hbm,
    gq_hbm, gp_hbm, loss_ref,
    q0, p0, pl_in, pr_in, xl_in, xr_in, tl_in, tr_in, send_r, send_l,
    s3, row_lse, col_lse, msg_l, msg_r, pos_t, w_row, wt_p, stage,
    sem_q, sem_p, ps_r, ps_l, pr_r, pr_l, xs_r, xs_l, xr_r, xr_l, ts_r, ts_l, tr_r, tr_l,
    msg_send, msg_recv, out_sem, token,
):
    pb, pa = lax.axis_index("pb"), lax.axis_index("pa")
    me = pb * PA + pa
    after = lax.rem(me + 1, NB)
    before = lax.rem(me + NB - 1, NB)
    right = (after // PA, lax.rem(after, PA))
    left = (before // PA, lax.rem(before, PA))

    core = lax.rem(pb, 2)
    twin = (pb + 1 - 2 * core, pa)

    barrier = pltpu.get_barrier_semaphore()
    for neighbour in (left, right, twin):
        pl.semaphore_signal(barrier, inc=1, device_id=neighbour, device_id_type=MESH)
    pl.semaphore_wait(barrier, 3)

    WAYS = ("r", "l")
    order = {
        "r": lax.rem(core + jnp.where(pa == PA - 1, 1, 0), 2),
        "l": lax.rem(core + jnp.where(pa == 0, 1, 0), 2),
    }
    mixed = jnp.logical_or(pa == PA - 1, pa == 0)
    give_at = jnp.where(mixed, NC - HOLD, NC - 1)

    def columns(c):
        return pl.ds(pl.multiple_of(c * CW, CW), CW)

    def remote(src, dst, send, recv, to):
        return pltpu.make_async_remote_copy(
            src_ref=src, dst_ref=dst, send_sem=send, recv_sem=recv, device_id=to, device_id_type=MESH
        )

    def p_right(c):
        return remote(p_hbm.at[:, columns(c)], pl_in.at[c], ps_r.at[c], pr_r.at[c], right)

    def p_left(c):
        return remote(p_hbm.at[:, columns(c)], pr_in.at[c], ps_l.at[c], pr_l.at[c], left)

    def x_right(c):
        return remote(send_r.at[c], xl_in.at[c], xs_r.at[c], xr_r.at[c], right)

    def x_left(c):
        return remote(send_l.at[c], xr_in.at[c], xs_l.at[c], xr_l.at[c], left)

    def t_right(c):
        return remote(send_r.at[c], tl_in.at[c], ts_r.at[c], tr_r.at[c], right)

    def t_left(c):
        return remote(send_l.at[c], tr_in.at[c], ts_l.at[c], tr_l.at[c], left)

    def q_load(c):
        return pltpu.make_async_copy(q_hbm.at[:, columns(c)], q0.at[c], sem_q.at[c])

    def p_load(c):
        return pltpu.make_async_copy(p_hbm.at[:, columns(c)], p0.at[c], sem_p.at[c])

    @pl.loop(0, NC)
    def _(c):
        p_right(c).start()
        p_left(c).start()
        q_load(c).start()
        p_load(c).start()

    def scan_sizes(k, carry):
        end, at_me, at_next, at_before, at_after = carry
        end = end + sizes_ref[k]
        one = jnp.int32(1)
        return (
            end,
            jnp.where(end == me, one, at_me),
            jnp.where(end == me + 1, one, at_next),
            jnp.where(end == me - 1, one, at_before),
            jnp.where(end == me + 2, one, at_after),
        )

    zero = jnp.int32(0)
    _, at_me, at_next, at_before, at_after = lax.fori_loop(0, NCL, scan_sizes, (zero,) * 5)
    has_l = jnp.where(me > 0, 1 - at_me, 0)
    has_r = jnp.where(me < NB - 1, 1 - at_next, 0)
    far_l = jnp.where(me > 1, 1 - at_before, 0) * has_l
    far_r = jnp.where(me < NB - 2, 1 - at_after, 0) * has_r
    rows_l = has_l - far_l
    rows_r = has_r - far_r

    def add_scores(r, k, c, a_ref, b_ref):
        for h in range(HALVES):
            ref = s3.at[pl.ds(r * BLK + h * HB, HB), pl.ds(k * BLK, BLK)]
            part = dot_nt(a_ref[c, h * HB:(h + 1) * HB, :], b_ref[c])

            @pl.when(c == 0)
            def _():
                ref[...] = part

            @pl.when(c > 0)
            def _():
                ref[...] += part

    @pl.loop(0, NC)
    def _(c):
        q_load(c).wait()
        p_load(c).wait()
        add_scores(1, 1, c, q0, p0)

    @pl.loop(0, NC)
    def _(c):
        p_right(c).wait_recv()
        p_left(c).wait_recv()
        for h in range(HALVES):
            here = slice(h * HB, (h + 1) * HB)
            send_r[c, here, :] = jnp.where(mask_of(has_l, (HB, CW)), pl_in[c, here, :], q0[c, here, :])
        @pl.when(jnp.logical_or(order["r"] == 0, c < NC - HOLD))
        def _():
            x_right(c).start()

        for h in range(HALVES):
            here = slice(h * HB, (h + 1) * HB)
            send_l[c, here, :] = jnp.where(mask_of(has_r, (HB, CW)), pr_in[c, here, :], q0[c, here, :])
        @pl.when(jnp.logical_or(order["l"] == 0, c < NC - HOLD))
        def _():
            x_left(c).start()

        add_scores(1, 0, c, q0, pl_in)
        add_scores(1, 2, c, q0, pr_in)

    send_x = {"r": x_right, "l": x_left}

    @pl.loop(0, NC)
    def _(c):
        for at, way in enumerate(WAYS):
            @pl.when(jnp.logical_and(c == give_at, order[way] == 0))
            def _():
                @pl.loop(0, NC - 1)
                def _(k):
                    send_x[way](k).wait_send()

                pl.semaphore_signal(token.at[at], inc=1, device_id=twin, device_id_type=MESH)

        for at, way in enumerate(WAYS):
            @pl.when(jnp.logical_and(c == NC - HOLD, order[way] == 1))
            def _():
                pl.semaphore_wait(token.at[at], 1)

                @pl.loop(NC - HOLD, NC)
                def _(k):
                    send_x[way](k).start()

        x_right(c).wait_recv()
        x_left(c).wait_recv()
        for r, x_in in ((0, xl_in), (2, xr_in)):
            for k, p_in in ((0, pl_in), (1, p0), (2, pr_in)):
                add_scores(r, k, c, x_in, p_in)

    held_rows = (rows_l, jnp.int32(1), rows_r)
    held_cols = (has_l, jnp.int32(1), has_r)
    RT = 64

    def valid(r, k, shape):
        return mask_of(held_rows[r] * held_cols[k], shape)

    col_peak = [jnp.full((8, BLK), LOWEST, F32) for _ in range(3)]
    for r in range(3):
        def peaks(t, peak):
            rows = pl.ds(pl.multiple_of(r * BLK + t * RT, RT), RT)
            tiles = [
                jnp.where(valid(r, k, (RT, BLK)), s3[rows, k * BLK:(k + 1) * BLK] * SCALE, LOWEST)
                for k in range(3)
            ]
            top = jnp.max(jnp.maximum(jnp.maximum(tiles[0], tiles[1]), tiles[2]), axis=1, keepdims=True)
            total = jnp.zeros((RT, 1), F32)
            for tile in tiles:
                total = total + jnp.sum(jnp.exp(tile - top), axis=1, keepdims=True)
            row_lse[rows, :] = jnp.broadcast_to(top + jnp.log(total), (RT, 128))
            return tuple(
                jnp.maximum(old, jnp.max(tile.reshape(RT // 8, 8, BLK), axis=0))
                for old, tile in zip(peak, tiles)
            )

        col_peak = lax.fori_loop(0, BLK // RT, peaks, tuple(col_peak))
    col_top = [jnp.max(peak, axis=0, keepdims=True) for peak in col_peak]
    col_sum = [jnp.zeros((8, BLK), F32) for _ in range(3)]
    for r in range(3):
        def sums(t, total):
            rows = pl.ds(pl.multiple_of(r * BLK + t * RT, RT), RT)
            out = []
            for k in range(3):
                tile = jnp.where(valid(r, k, (RT, BLK)), s3[rows, k * BLK:(k + 1) * BLK] * SCALE, LOWEST)
                part = jnp.exp(tile - col_top[k])
                out.append(total[k] + jnp.sum(part.reshape(RT // 8, 8, BLK), axis=0))
            return tuple(out)

        col_sum = lax.fori_loop(0, BLK // RT, sums, tuple(col_sum))
    for k in range(3):
        lse = col_top[k] + jnp.log(jnp.sum(col_sum[k], axis=0, keepdims=True))
        col_lse[:, k * BLK:(k + 1) * BLK] = jnp.broadcast_to(lse, (8, BLK))

    tell_r = remote(col_lse, msg_l, msg_send.at[0], msg_recv.at[0], right)
    tell_l = remote(col_lse, msg_r, msg_send.at[1], msg_recv.at[1], left)
    tell_r.start()
    tell_l.start()

    def weight_tile(tile, lse_rows, lse_cols):
        return jnp.exp(tile - lse_rows) + jnp.exp(tile - lse_cols)

    def weights_t(r, k, out, at):
        ok = held_rows[r] * held_cols[k]
        lse_cols = col_lse[0:1, k * BLK:(k + 1) * BLK]

        @pl.loop(0, 4)
        def _(t):
            rows = pl.ds(pl.multiple_of(r * BLK + t * 128, 128), 128)
            tile = s3[rows, k * BLK:(k + 1) * BLK] * SCALE
            value = weight_tile(tile, row_lse[rows, 0:1], lse_cols)
            value = jnp.where(mask_of(ok, value.shape), value, 0.0)
            out[:, pl.ds(pl.multiple_of(at + t * 128, 128), 128)] = value.T.astype(BF16)

    for place, (r, k) in enumerate(((1, 0), (2, 0), (1, 2), (0, 2))):
        weights_t(r, k, w_row, place * BLK)

    @pl.loop(0, NC)
    def _(c):
        @pl.when(jnp.logical_or(order["l"] == 1, c == NC - 1))
        def _():
            x_left(c).wait_send()

        for h in range(HALVES):
            here = slice(h * HB, (h + 1) * HB)
            term = dot_nn(w_row[here, :BLK], q0[c]) + dot_nn(w_row[here, BLK:2 * BLK], xr_in[c])
            send_l[c, here, :] = term.astype(BF16)
        t_left(c).start()
        @pl.when(jnp.logical_or(order["r"] == 1, c == NC - 1))
        def _():
            x_right(c).wait_send()

        for h in range(HALVES):
            here = slice(h * HB, (h + 1) * HB)
            term = dot_nn(w_row[here, 2 * BLK:3 * BLK], q0[c]) + dot_nn(w_row[here, 3 * BLK:], xl_in[c])
            send_r[c, here, :] = term.astype(BF16)
        t_right(c).start()

    @pl.loop(0, NC)
    def _(c):
        for h in range(HALVES):
            here = slice(h * HB, (h + 1) * HB)
            xl_in[c, here, :] = jnp.where(mask_of(far_r, (HB, CW)), xr_in[c, here, :], xl_in[c, here, :])
        add_scores(0, 0, c, q0, xl_in)

    tell_r.wait()
    tell_l.wait()
    end = far_l + far_r

    def pick(from_left, from_right, own):
        out = own
        if from_left is not None:
            out = jnp.where(mask_of(far_l, (1, BLK)), msg_l[0:1, from_left * BLK:(from_left + 1) * BLK], out)
        if from_right is not None:
            out = jnp.where(mask_of(far_r, (1, BLK)), msg_r[0:1, from_right * BLK:(from_right + 1) * BLK], out)
        return out

    own_cols = [col_lse[0:1, k * BLK:(k + 1) * BLK] for k in range(3)]
    lse_l = pick(1, None, own_cols[0])
    lse_0 = pick(2, 0, own_cols[1])
    lse_r = pick(None, 1, own_cols[2])
    lse_x = pick(0, 2, own_cols[0])
    pos_t[...] = jnp.broadcast_to(pos_ref[...].astype(F32), (128, BLK)).T
    flags = (has_l, jnp.int32(1), has_r, end)
    WT = 128

    @pl.loop(0, BLK // WT)
    def _(t):
        here = pl.ds(pl.multiple_of(t * WT, WT), WT)
        own = pl.ds(pl.multiple_of(BLK + t * WT, WT), WT)
        shape = (WT, BLK)
        raw = [s3[own, k * BLK:(k + 1) * BLK] * SCALE for k in range(3)] + [s3[here, :BLK] * SCALE]
        tiles = [jnp.where(mask_of(flag, shape), tile, LOWEST) for flag, tile in zip(flags, raw)]
        top = jnp.max(
            jnp.maximum(jnp.maximum(tiles[0], tiles[1]), jnp.maximum(tiles[2], tiles[3])), axis=1, keepdims=True
        )
        total = jnp.zeros((WT, 1), F32)
        for tile in tiles:
            total = total + jnp.sum(jnp.exp(tile - top), axis=1, keepdims=True)
        lse_rows = top + jnp.log(total)
        lane = lax.broadcasted_iota(jnp.int32, shape, 1).astype(F32)
        onehot = jnp.concatenate([pos_t[here, :]] * 4, axis=1) == lane
        hits = jnp.where(onehot, lse_0 - 2.0 * raw[1], 0.0)
        loss = lse_rows + jnp.sum(hits, axis=1, keepdims=True)
        loss_ref[:, here] = jnp.broadcast_to(loss, (WT, 128)).T[0:1, :]
        for k, (flag, tile, lse_cols) in enumerate(zip(flags, raw, (lse_l, lse_0, lse_r, lse_x))):
            value = weight_tile(tile, lse_rows, lse_cols)
            if k == 1:
                value = jnp.where(onehot, value - 2.0, value)
            value = jnp.where(mask_of(flag, shape), value, 0.0)
            w_row[here, k * BLK:(k + 1) * BLK] = value.astype(BF16)
            if k == 1:
                wt_p[:, here] = value.T.astype(BF16)

    weights_t(0, 1, wt_p, BLK)
    weights_t(2, 1, wt_p, 2 * BLK)

    def gq_out(c, slot):
        return pltpu.make_async_copy(stage.at[slot], gq_hbm.at[:, columns(c)], out_sem.at[slot])

    def gp_out(c, slot):
        return pltpu.make_async_copy(stage.at[slot], gp_hbm.at[:, columns(c)], out_sem.at[slot])

    @pl.loop(0, NC)
    def _(c):
        slot = lax.rem(c, 2)

        @pl.when(c >= 2)
        def _():
            gq_out(c - 2, slot).wait()

        for h in range(HALVES):
            here = slice(h * HB, (h + 1) * HB)
            total = dot_nn(w_row[here, :BLK], pl_in[c]) + dot_nn(w_row[here, BLK:2 * BLK], p0[c])
            total = total + dot_nn(w_row[here, 2 * BLK:3 * BLK], pr_in[c]) + dot_nn(w_row[here, 3 * BLK:], xl_in[c])
            stage[slot, here, :] = total.astype(BF16)
        gq_out(c, slot).start()

    @pl.loop(0, NC)
    def _(c):
        slot = lax.rem(c, 2)

        @pl.when(c < 2)
        def _():
            gq_out(NC - 2 + c, slot).wait()

        @pl.when(c >= 2)
        def _():
            gp_out(c - 2, slot).wait()

        shape = (HB, CW)
        totals = []
        for h in range(HALVES):
            here = slice(h * HB, (h + 1) * HB)
            total = dot_nn(wt_p[here, :BLK], q0[c]) + dot_nn(wt_p[here, BLK:2 * BLK], xl_in[c])
            totals.append(total + dot_nn(wt_p[here, 2 * BLK:], xr_in[c]))
        t_right(c).wait_recv()
        t_left(c).wait_recv()
        for h, total in enumerate(totals):
            here = slice(h * HB, (h + 1) * HB)
            total = total + jnp.where(mask_of(far_l, shape), tl_in[c, here, :].astype(F32), 0.0)
            total = total + jnp.where(mask_of(far_r, shape), tr_in[c, here, :].astype(F32), 0.0)
            stage[slot, here, :] = total.astype(BF16)
        gp_out(c, slot).start()

    for c in (NC - 2, NC - 1):
        gp_out(c, c % 2).wait()

    @pl.loop(0, NC)
    def _(c):
        p_right(c).wait_send()
        p_left(c).wait_send()
        t_right(c).wait_send()
        t_left(c).wait_send()


def per_device(queries, passages, cluster_sizes, positives):
    block = pltpu.VMEM((NC, BLK, CW), BF16)
    dma = pltpu.SemaphoreType.DMA
    any_space = pl.BlockSpec(memory_space=pl.ANY)
    in_vmem = pl.BlockSpec(memory_space=pltpu.VMEM)
    return pl.pallas_call(
        exchange_kernel,
        out_shape=(
            jax.ShapeDtypeStruct((BLK, D), BF16),
            jax.ShapeDtypeStruct((BLK, D), BF16),
            jax.ShapeDtypeStruct((1, BLK), F32),
        ),
        in_specs=[pl.BlockSpec(memory_space=pltpu.SMEM), in_vmem, any_space, any_space],
        out_specs=(any_space, any_space, in_vmem),
        scratch_shapes=[block] * 10
        + [
            pltpu.VMEM((3 * BLK, 3 * BLK), F32),
            pltpu.VMEM((3 * BLK, 128), F32),
            pltpu.VMEM((8, 3 * BLK), F32),
            pltpu.VMEM((8, 3 * BLK), F32),
            pltpu.VMEM((8, 3 * BLK), F32),
            pltpu.VMEM((BLK, 128), F32),
            pltpu.VMEM((BLK, 4 * BLK), BF16),
            pltpu.VMEM((BLK, 3 * BLK), BF16),
            pltpu.VMEM((2, BLK, CW), BF16),
        ]
        + [dma((NC,))] * 14
        + [dma((2,))] * 3
        + [pltpu.SemaphoreType.REGULAR((2,))],
        compiler_params=pltpu.CompilerParams(
            collective_id=0, has_side_effects=True, vmem_limit_bytes=VM * 1024 * 1024
        ),
        cost_estimate=pl.CostEstimate(flops=50_000_000_000, bytes_accessed=64 << 20, transcendentals=0),
    )(cluster_sizes, positives, queries, passages)


def solution(mesh):
    placed = (P(("pb", "pa"), None), P(("pb", "pa"), None), P(), P(("pb", "pa"), None))
    return jax.shard_map(
        per_device,
        mesh=mesh,
        in_specs=placed,
        out_specs=(P(("pb", "pa"), None), P(("pb", "pa"), None), P(("pb", "pa"), None)),
        check_vma=False,
    )
```

```python
import jax
import jax.numpy as jnp
from jax import lax
from jax.experimental import pallas as pl
from jax.experimental.pallas import tpu as pltpu
from jax.sharding import PartitionSpec as P

BLK = 512
D = 4096
NB = 128
NCL = 64
NC = 8
CW = D // NC
PA = 16
HALVES = 2
HOLD = 6
VM = 62
HB = BLK // HALVES
LOWEST = -1e30
SCALE = float(D) ** (-0.5)
F32 = jnp.float32
BF16 = jnp.bfloat16
MESH = pl.DeviceIdType.MESH


def dot_nt(a, b):
    return lax.dot_general(a, b, (((1,), (1,)), ((), ())), preferred_element_type=F32)


def dot_nn(a, b):
    return jnp.dot(a, b, preferred_element_type=F32)


def mask_of(flag, shape):
    return jnp.full(shape, flag, jnp.int32) > 0


def exchange_kernel(
    sizes_ref, pos_ref, q_hbm, p_hbm,
    gq_hbm, gp_hbm, loss_ref,
    q0, p0, pl_in, pr_in, xl_in, xr_in, tl_in, tr_in, send_r, send_l,
    s3, row_lse, col_lse, msg_l, msg_r, pos_t, w_row, wt_p, stage,
    sem_q, sem_p, ps_r, ps_l, pr_r, pr_l, xs_r, xs_l, xr_r, xr_l, ts_r, ts_l, tr_r, tr_l,
    msg_send, msg_recv, out_sem, token,
):
    pb, pa = lax.axis_index("pb"), lax.axis_index("pa")
    me = pb * PA + pa
    after = lax.rem(me + 1, NB)
    before = lax.rem(me + NB - 1, NB)
    right = (after // PA, lax.rem(after, PA))
    left = (before // PA, lax.rem(before, PA))

    core = lax.rem(pb, 2)
    twin = (pb + 1 - 2 * core, pa)

    barrier = pltpu.get_barrier_semaphore()
    for neighbour in (left, right, twin):
        pl.semaphore_signal(barrier, inc=1, device_id=neighbour, device_id_type=MESH)

    @pl.loop(0, NC)
    def _(c):
        here = pl.ds(pl.multiple_of(c * CW, CW), CW)
        pltpu.make_async_copy(q_hbm.at[:, here], q0.at[c], sem_q.at[c]).start()
        pltpu.make_async_copy(p_hbm.at[:, here], p0.at[c], sem_p.at[c]).start()

    pl.semaphore_wait(barrier, 3)

    WAYS = ("r", "l")
    order = {
        "r": lax.rem(core + jnp.where(pa == PA - 1, 1, 0), 2),
        "l": lax.rem(core + jnp.where(pa == 0, 1, 0), 2),
    }
    mixed = jnp.logical_or(pa == PA - 1, pa == 0)
    give_at = jnp.where(mixed, NC - HOLD, NC - 1)

    def columns(c):
        return pl.ds(pl.multiple_of(c * CW, CW), CW)

    def remote(src, dst, send, recv, to):
        return pltpu.make_async_remote_copy(
            src_ref=src, dst_ref=dst, send_sem=send, recv_sem=recv, device_id=to, device_id_type=MESH
        )

    def p_right(c):
        return remote(p_hbm.at[:, columns(c)], pl_in.at[c], ps_r.at[c], pr_r.at[c], right)

    def p_left(c):
        return remote(p_hbm.at[:, columns(c)], pr_in.at[c], ps_l.at[c], pr_l.at[c], left)

    def x_right(c):
        return remote(send_r.at[c], xl_in.at[c], xs_r.at[c], xr_r.at[c], right)

    def x_left(c):
        return remote(send_l.at[c], xr_in.at[c], xs_l.at[c], xr_l.at[c], left)

    def t_right(c):
        return remote(send_r.at[c], tl_in.at[c], ts_r.at[c], tr_r.at[c], right)

    def t_left(c):
        return remote(send_l.at[c], tr_in.at[c], ts_l.at[c], tr_l.at[c], left)

    def q_load(c):
        return pltpu.make_async_copy(q_hbm.at[:, columns(c)], q0.at[c], sem_q.at[c])

    def p_load(c):
        return pltpu.make_async_copy(p_hbm.at[:, columns(c)], p0.at[c], sem_p.at[c])

    @pl.loop(0, NC)
    def _(c):
        p_right(c).start()
        p_left(c).start()

    def scan_sizes(k, carry):
        end, at_me, at_next, at_before, at_after = carry
        end = end + sizes_ref[k]
        one = jnp.int32(1)
        return (
            end,
            jnp.where(end == me, one, at_me),
            jnp.where(end == me + 1, one, at_next),
            jnp.where(end == me - 1, one, at_before),
            jnp.where(end == me + 2, one, at_after),
        )

    zero = jnp.int32(0)
    _, at_me, at_next, at_before, at_after = lax.fori_loop(0, NCL, scan_sizes, (zero,) * 5)
    has_l = jnp.where(me > 0, 1 - at_me, 0)
    has_r = jnp.where(me < NB - 1, 1 - at_next, 0)
    far_l = jnp.where(me > 1, 1 - at_before, 0) * has_l
    far_r = jnp.where(me < NB - 2, 1 - at_after, 0) * has_r
    rows_l = has_l - far_l
    rows_r = has_r - far_r

    def add_scores(r, k, c, a_ref, b_ref):
        for h in range(HALVES):
            ref = s3.at[pl.ds(r * BLK + h * HB, HB), pl.ds(k * BLK, BLK)]
            part = dot_nt(a_ref[c, h * HB:(h + 1) * HB, :], b_ref[c])

            @pl.when(c == 0)
            def _():
                ref[...] = part

            @pl.when(c > 0)
            def _():
                ref[...] += part

    @pl.loop(0, NC)
    def _(c):
        q_load(c).wait()
        p_load(c).wait()
        add_scores(1, 1, c, q0, p0)

    @pl.loop(0, NC)
    def _(c):
        p_right(c).wait_recv()
        p_left(c).wait_recv()
        for h in range(HALVES):
            here = slice(h * HB, (h + 1) * HB)
            send_r[c, here, :] = jnp.where(mask_of(has_l, (HB, CW)), pl_in[c, here, :], q0[c, here, :])
        @pl.when(jnp.logical_or(order["r"] == 0, c < NC - HOLD))
        def _():
            x_right(c).start()

        for h in range(HALVES):
            here = slice(h * HB, (h + 1) * HB)
            send_l[c, here, :] = jnp.where(mask_of(has_r, (HB, CW)), pr_in[c, here, :], q0[c, here, :])
        @pl.when(jnp.logical_or(order["l"] == 0, c < NC - HOLD))
        def _():
            x_left(c).start()

        add_scores(1, 0, c, q0, pl_in)
        add_scores(1, 2, c, q0, pr_in)

    send_x = {"r": x_right, "l": x_left}

    @pl.loop(0, NC)
    def _(c):
        for at, way in enumerate(WAYS):
            @pl.when(jnp.logical_and(c == give_at, order[way] == 0))
            def _():
                @pl.loop(0, NC - 1)
                def _(k):
                    send_x[way](k).wait_send()

                pl.semaphore_signal(token.at[at], inc=1, device_id=twin, device_id_type=MESH)

        for at, way in enumerate(WAYS):
            @pl.when(jnp.logical_and(c == NC - HOLD, order[way] == 1))
            def _():
                pl.semaphore_wait(token.at[at], 1)

                @pl.loop(NC - HOLD, NC)
                def _(k):
                    send_x[way](k).start()

        x_right(c).wait_recv()
        x_left(c).wait_recv()
        for r, x_in in ((0, xl_in), (2, xr_in)):
            for k, p_in in ((0, pl_in), (1, p0), (2, pr_in)):
                add_scores(r, k, c, x_in, p_in)

    held_rows = (rows_l, jnp.int32(1), rows_r)
    held_cols = (has_l, jnp.int32(1), has_r)
    RT = 64

    def valid(r, k, shape):
        return mask_of(held_rows[r] * held_cols[k], shape)

    col_peak = [jnp.full((8, BLK), LOWEST, F32) for _ in range(3)]
    for r in range(3):
        def peaks(t, peak):
            rows = pl.ds(pl.multiple_of(r * BLK + t * RT, RT), RT)
            tiles = [
                jnp.where(valid(r, k, (RT, BLK)), s3[rows, k * BLK:(k + 1) * BLK] * SCALE, LOWEST)
                for k in range(3)
            ]
            top = jnp.max(jnp.maximum(jnp.maximum(tiles[0], tiles[1]), tiles[2]), axis=1, keepdims=True)
            total = jnp.zeros((RT, 1), F32)
            for tile in tiles:
                total = total + jnp.sum(jnp.exp(tile - top), axis=1, keepdims=True)
            row_lse[rows, :] = jnp.broadcast_to(top + jnp.log(total), (RT, 128))
            return tuple(
                jnp.maximum(old, jnp.max(tile.reshape(RT // 8, 8, BLK), axis=0))
                for old, tile in zip(peak, tiles)
            )

        col_peak = lax.fori_loop(0, BLK // RT, peaks, tuple(col_peak))
    col_top = [jnp.max(peak, axis=0, keepdims=True) for peak in col_peak]
    col_sum = [jnp.zeros((8, BLK), F32) for _ in range(3)]
    for r in range(3):
        def sums(t, total):
            rows = pl.ds(pl.multiple_of(r * BLK + t * RT, RT), RT)
            out = []
            for k in range(3):
                tile = jnp.where(valid(r, k, (RT, BLK)), s3[rows, k * BLK:(k + 1) * BLK] * SCALE, LOWEST)
                part = jnp.exp(tile - col_top[k])
                out.append(total[k] + jnp.sum(part.reshape(RT // 8, 8, BLK), axis=0))
            return tuple(out)

        col_sum = lax.fori_loop(0, BLK // RT, sums, tuple(col_sum))
    for k in range(3):
        lse = col_top[k] + jnp.log(jnp.sum(col_sum[k], axis=0, keepdims=True))
        col_lse[:, k * BLK:(k + 1) * BLK] = jnp.broadcast_to(lse, (8, BLK))

    tell_r = remote(col_lse, msg_l, msg_send.at[0], msg_recv.at[0], right)
    tell_l = remote(col_lse, msg_r, msg_send.at[1], msg_recv.at[1], left)
    tell_r.start()
    tell_l.start()

    def weight_tile(tile, lse_rows, lse_cols):
        return jnp.exp(tile - lse_rows) + jnp.exp(tile - lse_cols)

    def weights_t(r, k, out, at):
        ok = held_rows[r] * held_cols[k]
        lse_cols = col_lse[0:1, k * BLK:(k + 1) * BLK]

        @pl.loop(0, 4)
        def _(t):
            rows = pl.ds(pl.multiple_of(r * BLK + t * 128, 128), 128)
            tile = s3[rows, k * BLK:(k + 1) * BLK] * SCALE
            value = weight_tile(tile, row_lse[rows, 0:1], lse_cols)
            value = jnp.where(mask_of(ok, value.shape), value, 0.0)
            out[:, pl.ds(pl.multiple_of(at + t * 128, 128), 128)] = value.T.astype(BF16)

    for place, (r, k) in enumerate(((1, 0), (2, 0), (1, 2), (0, 2))):
        weights_t(r, k, w_row, place * BLK)

    @pl.loop(0, NC)
    def _(c):
        @pl.when(jnp.logical_or(order["l"] == 1, c == NC - 1))
        def _():
            x_left(c).wait_send()

        for h in range(HALVES):
            here = slice(h * HB, (h + 1) * HB)
            term = dot_nn(w_row[here, :BLK], q0[c]) + dot_nn(w_row[here, BLK:2 * BLK], xr_in[c])
            send_l[c, here, :] = term.astype(BF16)
        t_left(c).start()
        @pl.when(jnp.logical_or(order["r"] == 1, c == NC - 1))
        def _():
            x_right(c).wait_send()

        for h in range(HALVES):
            here = slice(h * HB, (h + 1) * HB)
            term = dot_nn(w_row[here, 2 * BLK:3 * BLK], q0[c]) + dot_nn(w_row[here, 3 * BLK:], xl_in[c])
            send_r[c, here, :] = term.astype(BF16)
        t_right(c).start()

    @pl.loop(0, NC)
    def _(c):
        for h in range(HALVES):
            here = slice(h * HB, (h + 1) * HB)
            xl_in[c, here, :] = jnp.where(mask_of(far_r, (HB, CW)), xr_in[c, here, :], xl_in[c, here, :])
        add_scores(0, 0, c, q0, xl_in)

    tell_r.wait()
    tell_l.wait()
    end = far_l + far_r

    def pick(from_left, from_right, own):
        out = own
        if from_left is not None:
            out = jnp.where(mask_of(far_l, (1, BLK)), msg_l[0:1, from_left * BLK:(from_left + 1) * BLK], out)
        if from_right is not None:
            out = jnp.where(mask_of(far_r, (1, BLK)), msg_r[0:1, from_right * BLK:(from_right + 1) * BLK], out)
        return out

    own_cols = [col_lse[0:1, k * BLK:(k + 1) * BLK] for k in range(3)]
    lse_l = pick(1, None, own_cols[0])
    lse_0 = pick(2, 0, own_cols[1])
    lse_r = pick(None, 1, own_cols[2])
    lse_x = pick(0, 2, own_cols[0])
    pos_t[...] = jnp.broadcast_to(pos_ref[...].astype(F32), (128, BLK)).T
    flags = (has_l, jnp.int32(1), has_r, end)
    WT = 128

    @pl.loop(0, BLK // WT)
    def _(t):
        here = pl.ds(pl.multiple_of(t * WT, WT), WT)
        own = pl.ds(pl.multiple_of(BLK + t * WT, WT), WT)
        shape = (WT, BLK)
        raw = [s3[own, k * BLK:(k + 1) * BLK] * SCALE for k in range(3)] + [s3[here, :BLK] * SCALE]
        tiles = [jnp.where(mask_of(flag, shape), tile, LOWEST) for flag, tile in zip(flags, raw)]
        top = jnp.max(
            jnp.maximum(jnp.maximum(tiles[0], tiles[1]), jnp.maximum(tiles[2], tiles[3])), axis=1, keepdims=True
        )
        total = jnp.zeros((WT, 1), F32)
        for tile in tiles:
            total = total + jnp.sum(jnp.exp(tile - top), axis=1, keepdims=True)
        lse_rows = top + jnp.log(total)
        lane = lax.broadcasted_iota(jnp.int32, shape, 1).astype(F32)
        onehot = jnp.concatenate([pos_t[here, :]] * 4, axis=1) == lane
        hits = jnp.where(onehot, lse_0 - 2.0 * raw[1], 0.0)
        loss = lse_rows + jnp.sum(hits, axis=1, keepdims=True)
        loss_ref[:, here] = jnp.broadcast_to(loss, (WT, 128)).T[0:1, :]
        for k, (flag, tile, lse_cols) in enumerate(zip(flags, raw, (lse_l, lse_0, lse_r, lse_x))):
            value = weight_tile(tile, lse_rows, lse_cols)
            if k == 1:
                value = jnp.where(onehot, value - 2.0, value)
            value = jnp.where(mask_of(flag, shape), value, 0.0)
            w_row[here, k * BLK:(k + 1) * BLK] = value.astype(BF16)
            if k == 1:
                wt_p[:, here] = value.T.astype(BF16)

    weights_t(0, 1, wt_p, BLK)
    weights_t(2, 1, wt_p, 2 * BLK)

    def gq_out(c, slot):
        return pltpu.make_async_copy(stage.at[slot], gq_hbm.at[:, columns(c)], out_sem.at[slot])

    def gp_out(c, slot):
        return pltpu.make_async_copy(stage.at[slot], gp_hbm.at[:, columns(c)], out_sem.at[slot])

    @pl.loop(0, NC)
    def _(c):
        slot = lax.rem(c, 2)

        @pl.when(c >= 2)
        def _():
            gq_out(c - 2, slot).wait()

        for h in range(HALVES):
            here = slice(h * HB, (h + 1) * HB)
            total = dot_nn(w_row[here, :BLK], pl_in[c]) + dot_nn(w_row[here, BLK:2 * BLK], p0[c])
            total = total + dot_nn(w_row[here, 2 * BLK:3 * BLK], pr_in[c]) + dot_nn(w_row[here, 3 * BLK:], xl_in[c])
            stage[slot, here, :] = total.astype(BF16)
        gq_out(c, slot).start()

    @pl.loop(0, NC)
    def _(c):
        slot = lax.rem(c, 2)

        @pl.when(c < 2)
        def _():
            gq_out(NC - 2 + c, slot).wait()

        @pl.when(c >= 2)
        def _():
            gp_out(c - 2, slot).wait()

        shape = (HB, CW)
        totals = []
        for h in range(HALVES):
            here = slice(h * HB, (h + 1) * HB)
            total = dot_nn(wt_p[here, :BLK], q0[c]) + dot_nn(wt_p[here, BLK:2 * BLK], xl_in[c])
            totals.append(total + dot_nn(wt_p[here, 2 * BLK:], xr_in[c]))
        t_right(c).wait_recv()
        t_left(c).wait_recv()
        for h, total in enumerate(totals):
            here = slice(h * HB, (h + 1) * HB)
            total = total + jnp.where(mask_of(far_l, shape), tl_in[c, here, :].astype(F32), 0.0)
            total = total + jnp.where(mask_of(far_r, shape), tr_in[c, here, :].astype(F32), 0.0)
            stage[slot, here, :] = total.astype(BF16)
        gp_out(c, slot).start()

    for c in (NC - 2, NC - 1):
        gp_out(c, c % 2).wait()

    @pl.loop(0, NC)
    def _(c):
        p_right(c).wait_send()
        p_left(c).wait_send()
        t_right(c).wait_send()
        t_left(c).wait_send()


def per_device(queries, passages, cluster_sizes, positives):
    block = pltpu.VMEM((NC, BLK, CW), BF16)
    dma = pltpu.SemaphoreType.DMA
    any_space = pl.BlockSpec(memory_space=pl.ANY)
    in_vmem = pl.BlockSpec(memory_space=pltpu.VMEM)
    return pl.pallas_call(
        exchange_kernel,
        out_shape=(
            jax.ShapeDtypeStruct((BLK, D), BF16),
            jax.ShapeDtypeStruct((BLK, D), BF16),
            jax.ShapeDtypeStruct((1, BLK), F32),
        ),
        in_specs=[pl.BlockSpec(memory_space=pltpu.SMEM), in_vmem, any_space, any_space],
        out_specs=(any_space, any_space, in_vmem),
        scratch_shapes=[block] * 10
        + [
            pltpu.VMEM((3 * BLK, 3 * BLK), F32),
            pltpu.VMEM((3 * BLK, 128), F32),
            pltpu.VMEM((8, 3 * BLK), F32),
            pltpu.VMEM((8, 3 * BLK), F32),
            pltpu.VMEM((8, 3 * BLK), F32),
            pltpu.VMEM((BLK, 128), F32),
            pltpu.VMEM((BLK, 4 * BLK), BF16),
            pltpu.VMEM((BLK, 3 * BLK), BF16),
            pltpu.VMEM((2, BLK, CW), BF16),
        ]
        + [dma((NC,))] * 14
        + [dma((2,))] * 3
        + [pltpu.SemaphoreType.REGULAR((2,))],
        compiler_params=pltpu.CompilerParams(
            collective_id=0, has_side_effects=True, vmem_limit_bytes=VM * 1024 * 1024
        ),
        cost_estimate=pl.CostEstimate(flops=50_000_000_000, bytes_accessed=64 << 20, transcendentals=0),
    )(cluster_sizes, positives, queries, passages)


def solution(mesh):
    placed = (P(("pb", "pa"), None), P(("pb", "pa"), None), P(), P(("pb", "pa"), None))
    return jax.shard_map(
        per_device,
        mesh=mesh,
        in_specs=placed,
        out_specs=(P(("pb", "pa"), None), P(("pb", "pa"), None), P(("pb", "pa"), None)),
        check_vma=False,
    )
```
